256 devices in a mesh: row: 8 (over z), col: 32 (over x, y, core).
Axes of the slice: x: 4, y: 4, z: 8, core: 2. Of those that a mesh axis runs over, the one named last changes fastest.
Arguments:
- rhs: float32 [4, 128, 1024, 64], P(None, 'row', 'col'), may hold values from -6 to 6
- dinv: float32 [4, 1024, 128, 128], P(None, 'col', 'row'), as said below
- panels: float32 [4, 8, 1024, 128, 128], P(None, None, 'col', 'row'), may hold values from -0.25 to 0.25
- pattern: int32 [4, 7, 1024], P(None, None, 'col'), may hold values 0 or 1
- parent_owner: int32 [3, 1024, 1], P(None, 'col'), may hold values from 0 to 31; in each aligned block of 32 rows (0 to 31, 32 to 63, ..., all dimensions but the last counted through in order) at most 2 rows name the same one
- parent_local: int32 [3, 1024], P(None, 'col'), may hold values from 0 to 31
- ancestor_solution: float32 [128, 1024, 8, 64], P('row', 'col'), may hold values from -6 to 6
Outputs:
- solution: float32 [4, 128, 1024, 64], P(None, 'row', 'col')
- boundary_update: float32 [128, 1024, 8, 64], P('row', 'col')
The draws below stay inside these ranges and needn't reach their ends.
Inputs may be any that keep to these rules, and one draw needn't show every extreme that they name: `dinv`: each block is lower triangular with a positive diagonal. `parent_owner`: among the supernodes of one level on one index of col, at most 2 have their parent on the same index of col, and some index of col reaches 2.
All inputs are finite; a program needn't handle non-finite values. No bound on the sum of `pattern` on one device may be relied on, other than what follows from the above.
Results may differ from the reference program's by a relative error of at most 0.0001.
Values sent between devices are 32-bit elements; how exact they have to be, the bound alone decides.
A program may use at most 128 MiB of HBM per device.

```python
import math
import jax
import jax.numpy as jnp
import numpy as np
from jax import lax

BLOCK = 128
RHS_COLS = 64
ANCESTORS = 8
LEVELS = 4
SUPER_COL = 32
SUPERNODES = 1024
CAPACITY = 2
N_COL = 32


def draw_dinv(key, part):
    key = jax.random.fold_in(key, 11)
    first, second = jax.random.split(key)
    shape = (LEVELS, SUPERNODES, BLOCK, BLOCK)
    row_ids = jnp.arange(BLOCK, dtype=jnp.int32)[:, None]
    col_ids = jnp.arange(BLOCK, dtype=jnp.int32)[None, :]
    lower = (col_ids < row_ids)[None, None, :, :]
    diagonal_mark = (col_ids == row_ids)[None, None, :, :]
    below = jax.random.normal(first, shape, jnp.float32) * (0.6 / BLOCK ** 0.5)
    diagonal = jax.random.uniform(second, shape[:3], jnp.float32, 0.5, 1.5)
    return jnp.where(lower, below, 0.0) + jnp.where(diagonal_mark, diagonal[..., None], 0.0)


def with_ends(result, own_key, low, high):
    longest = result.shape.index(max(result.shape))
    spots = []
    for shift in (0, 1):
        where = [jax.random.randint(jax.random.fold_in(own_key, axis), (), 0, length) for axis, length in enumerate(result.shape)]
        where[longest] = (where[longest] + shift) % result.shape[longest]
        spots.append(tuple(where))
    return result.at[spots[0]].set(low).at[spots[1]].set(high)


def levels(key, extent, pieces, least, high):
    def one(dim, blocks):
        steps = jax.random.uniform(jax.random.fold_in(jax.random.fold_in(key, 6), dim), (blocks,), jnp.float32, least / len(pieces), high / len(pieces))
        return jnp.repeat(jnp.exp(steps), extent[dim] // blocks).reshape((-1,) + (1,) * (len(extent) - dim - 1))

    factor_of = one(*pieces[0])
    for cut in pieces[1:]:
        factor_of = factor_of * one(*cut)
    return factor_of


def routed_block(rng, own, number, rows, number_of, top, reach, lean):
    ranking = jax.random.permutation(rng, number_of)
    crowded, ordinary = load_shares(number_of, rows * top, reach, lean, True), load_shares(number_of, rows * top, reach, lean, False)
    places = jnp.arange(number_of)

    def named(tallies, turn):
        used = int((tallies > 0).sum())
        fixed = max(1, used // 4)
        shifted = fixed + (places - fixed + turn * (used - fixed)) % max(1, number_of - fixed)
        return jnp.zeros((number_of,), jnp.int32).at[ranking[jnp.where(places < fixed, places, shifted)]].set(jnp.asarray(tallies, jnp.int32))

    tallies = jnp.where(number % 4 == 0, named(crowded, number // 4), named(ordinary, number - number // 4 - 1))
    mixed = jax.random.permutation(jax.random.fold_in(own, 3), number_of)
    donor, sink = mixed[0:number_of // 2 * 2:2], mixed[1:number_of // 2 * 2:2]
    margin = jnp.minimum(tallies[donor] - 1, reach - tallies[sink]) // 2
    margin = jnp.where((donor == ranking[0]) | (sink == ranking[0]) | (tallies[sink] == 0), 0, jnp.maximum(margin, 0))
    shifted = jax.random.randint(jax.random.fold_in(own, 4), (number_of // 2,), 0, 1 << 20) % (margin + 1)
    tallies = tallies.at[donor].add(-shifted).at[sink].add(shifted)
    items = jnp.searchsorted(jnp.cumsum(tallies), jnp.arange(rows * top), side="right").astype(jnp.int32)
    listing = items.reshape(top, rows).T
    listing = listing[jax.random.permutation(jax.random.fold_in(own, 1), rows)]
    turn = jax.random.randint(jax.random.fold_in(own, 2), (rows, 1), 0, top)
    return jnp.take_along_axis(listing, (jnp.arange(top)[None, :] + turn) % top, axis=1)


def load_shares(count, total, most, lean, full):
    weights = [(1 << 20) // math.isqrt(standing ** lean) + 1 for standing in range(1, count + 1)]
    largest = most if full else min(most, max(-(-total // count), total * weights[0] // sum(weights)))
    least = 1 if total - largest >= count - 1 else 0
    given, surplus = [largest] + [least] * (count - 1), total - largest - least * (count - 1)
    while surplus > 0:
        free = [i for i in range(1, count) if given[i] < largest] or [i for i in range(1, count) if given[i] < most]
        mass, left = sum([weights[i] for i in free]), surplus
        for i in free:
            more = min(most - given[i], max(1, left * weights[i] // mass), surplus)
            given[i] = given[i] + more
            surplus = surplus - more
    return np.array(given)


def centred(stream_key, extent, scale, most, cuts=(), kind=jnp.bfloat16):
    entries = scale * jax.random.normal(stream_key, extent, jnp.float32)
    if cuts:
        entries = entries * levels(stream_key, extent, cuts, -0.22, 0.18)
    return jnp.clip(entries, -most, most).astype(kind)


def setup_inputs(seed: int = 0) -> dict:
    streams_of = jax.random.split(jax.random.key(seed), 8)
    rhs = centred(streams_of[0], (LEVELS, BLOCK, SUPERNODES, RHS_COLS), 1.0, 6.0, ((1, 8), (2, 32)), jnp.float32)
    dinv = draw_dinv(jax.random.fold_in(streams_of[7], 71), 0)
    panels = centred(streams_of[2], (LEVELS, ANCESTORS, SUPERNODES, BLOCK, BLOCK), (4 * BLOCK) ** -0.5, 0.25, ((2, 32), (3, 8)), jnp.float32)
    pattern = with_ends((jax.random.randint(streams_of[3], (LEVELS, ANCESTORS - 1, SUPERNODES), 0, 4) < 3).astype(jnp.int32), jax.random.fold_in(streams_of[3], 1), 0, 1)
    parent_owner_keys = jax.random.split(jax.random.fold_in(streams_of[4], 1), (LEVELS - 1) * SUPERNODES // SUPER_COL)
    parent_owner_turns = jax.random.permutation(jax.random.fold_in(streams_of[4], 3), (LEVELS - 1) * SUPERNODES // SUPER_COL)
    parent_owner = jax.vmap(lambda own, number: routed_block(jax.random.fold_in(streams_of[4], 2), own, number, SUPER_COL, N_COL, 1, CAPACITY, 2))(parent_owner_keys, parent_owner_turns).reshape((LEVELS - 1, SUPERNODES, 1))
    parent_local = with_ends(jax.random.randint(streams_of[5], (LEVELS - 1, SUPERNODES), 0, SUPER_COL), jax.random.fold_in(streams_of[5], 1), 0, SUPER_COL - 1).astype(jnp.int32)
    ancestor_solution = centred(streams_of[6], (BLOCK, SUPERNODES, ANCESTORS, RHS_COLS), 1.0, 6.0, ((0, 8), (1, 32)), jnp.float32)
    return {"rhs": rhs, "dinv": dinv, "panels": panels, "pattern": pattern, "parent_owner": parent_owner, "parent_local": parent_local, "ancestor_solution": ancestor_solution}


def level_mask(pattern, height):
    return jnp.concatenate([jnp.ones((SUPERNODES, 1), jnp.float32), pattern[height].T.astype(jnp.float32)], axis=1)


def reference(rhs, dinv, panels, pattern, parent_owner, parent_local, ancestor_solution):
    highest = lax.Precision.HIGHEST
    width = ANCESTORS * RHS_COLS
    parents = (parent_owner[:, :, 0] * SUPER_COL + parent_local).astype(jnp.int32)
    child_sum = jnp.zeros((BLOCK, SUPERNODES, RHS_COLS), jnp.float32)
    carried = jnp.zeros((BLOCK, SUPERNODES, width), jnp.float32)
    solved = []
    outgoing = carried
    for height in range(LEVELS):
        block_mask = level_mask(pattern, height)
        solved_now = jnp.einsum("kib,bkr->ikr", dinv[height], rhs[height] - child_sum, precision=highest)
        solved.append(solved_now)
        product = jnp.einsum("dkib,bkr->ikdr", panels[height], solved_now, precision=highest)
        outgoing = (product * block_mask[None, :, :, None]).reshape(BLOCK, SUPERNODES, width) + carried
        if height < LEVELS - 1:
            summed = jax.ops.segment_sum(jnp.swapaxes(outgoing, 0, 1), parents[height], num_segments=SUPERNODES)
            summed = jnp.swapaxes(summed, 0, 1)
            child_sum = summed[:, :, :RHS_COLS]
            carried = jnp.concatenate([summed[:, :, RHS_COLS:], jnp.zeros_like(child_sum)], axis=2)
    boundary_update = outgoing.reshape(BLOCK, SUPERNODES, ANCESTORS, RHS_COLS)
    ancestry = ancestor_solution.reshape(BLOCK, SUPERNODES, width)
    results = [None] * LEVELS
    for height in reversed(range(LEVELS)):
        if height < LEVELS - 1:
            above = jnp.concatenate([results[height + 1], ancestry[:, :, :width - RHS_COLS]], axis=2)
            ancestry = jnp.take(above, parents[height], axis=1)
        block_mask = level_mask(pattern, height)
        masked = ancestry.reshape(BLOCK, SUPERNODES, ANCESTORS, RHS_COLS) * block_mask[None, :, :, None]
        reduced = solved[height] - jnp.einsum("dkib,ikdr->bkr", panels[height], masked, precision=highest)
        results[height] = jnp.einsum("kic,ikr->ckr", dinv[height], reduced, precision=highest)
    return jnp.stack(results), boundary_update
```

```python
import functools

import jax
import jax.numpy as jnp
from jax import lax
from jax.experimental import pallas as pl
from jax.experimental.pallas import tpu as pltpu
from jax.sharding import PartitionSpec as P

F32 = jnp.float32
BF16 = jnp.bfloat16
LEVELS = 4
ANC = 8
SUP = 32
SLOTS = 64
NR = 8
OWN = SUP // NR
FWD_GROUPS = ((0, 1), (1, 2), (2, 8))
BWD_GROUPS = (((0, 1), (1, 2), (2, 3), (3, 8)), ((0, 1), (1, 2), (2, 8)), ((0, 1), (1, 8)))
FSRC, POS, PREV, LAST, BSRC = range(5)


def low_lanes(shape):
    return lax.broadcasted_iota(jnp.int32, shape, len(shape) - 1) < 64


def swap_halves(x):
    return pltpu.roll(x.reshape(-1, 128), 64, 1).reshape(x.shape)


def split(x):
    high = x.astype(BF16).astype(F32)
    return high, x - high


def store_matrix(block):
    wide = jnp.concatenate([block[:8], block[8:]], axis=1)
    high, low = split(wide)
    return jnp.concatenate([high, low], axis=0).astype(BF16)


def expand(packed):
    low = low_lanes((8, 128))
    rolled = swap_halves(packed)
    zero = jnp.zeros((8, 128), F32)
    top, bottom = [], []
    for z in range(8):
        top += [jnp.where(low, packed[z], zero), jnp.where(low, rolled[z], zero)]
        bottom += [jnp.where(low, zero, rolled[z]), jnp.where(low, zero, packed[z])]
    high, rest = split(jnp.concatenate(top + bottom, axis=0))
    return jnp.concatenate([high.astype(BF16), rest.astype(BF16)], axis=1)


def apply(matrix, weights):
    o = jnp.dot(matrix, weights, preferred_element_type=F32).reshape(8, 2, 8, 256)
    return o[:, 0, :, :128] + o[:, 0, :, 128:] + o[:, 1, :, :128]


def apply_t(matrix, tiles):
    count = tiles.shape[0]
    high, rest = split(tiles)
    zero = jnp.zeros((8, 128), F32)
    rows = []
    for d in range(count):
        rows.append(jnp.concatenate([high[d], rest[d]], axis=1))
        rows.append(jnp.concatenate([high[d], zero], axis=1))
    weights = jnp.concatenate(rows, axis=0).astype(BF16)
    o = lax.dot_general(matrix, weights, (((0,), (0,)), ((), ())), preferred_element_type=F32)
    c = (o[:, :128] + o[:, 128:]).reshape(2, 8, 2, 8, 128)
    low = low_lanes((8, 8, 128))
    direct = jnp.where(low, c[0, :, 0], c[1, :, 1])
    cross = jnp.where(low, c[0, :, 1], c[1, :, 0])
    return direct + swap_halves(cross)


def kernel(
    ncol, tab, pat, rhs, anc, dinv, panels, sol_out, bu_out,
    stage, ph, dv, dh, rsend, rs, sol, out, car, cum, fsend, frecv, bsend, brecv, anct,
    part, rsr, tot, xsend, solr,
    sem_stage, sem_dv, sem_r, sem_ag_s, sem_ag_r, sem_fs, sem_fr, sem_bs, sem_br, sem_rs_s, sem_rs_r, sem_x,
):
    row, col = lax.axis_index("row"), lax.axis_index("col")
    cap = SLOTS // ncol
    right, left = lax.rem(row + 1, NR), lax.rem(row + NR - 1, NR)

    def rowdev(z):
        return {"row": z}

    def at_row(offset):
        return lax.rem(row + offset + 2 * NR, NR)

    barrier = pltpu.get_barrier_semaphore()

    @pl.loop(1, NR)
    def _(k):
        pl.semaphore_signal(barrier, inc=1, device_id=rowdev(lax.rem(row + k, NR)), device_id_type=pl.DeviceIdType.MESH)

    @pl.loop(1, ncol)
    def _(k):
        pl.semaphore_signal(barrier, inc=1, device_id={"col": lax.rem(col + k, ncol)}, device_id_type=pl.DeviceIdType.MESH)

    def load_panels(l):
        return pltpu.make_async_copy(panels.at[l], stage.at[l % 2], sem_stage.at[l % 2])

    load_panels(0).start()
    load_panels(1).start()
    pl.semaphore_wait(barrier, NR - 1 + ncol - 1)

    def row_send(src, dst, send_sem, recv_sem):
        @pl.loop(1, NR)
        def _(k):
            z = lax.rem(row + k, NR)
            pltpu.make_async_remote_copy(
                src_ref=src(z), dst_ref=dst(row), send_sem=send_sem, recv_sem=recv_sem,
                device_id=rowdev(z), device_id_type=pl.DeviceIdType.MESH,
            ).start()

    def wait_bytes(ref, sem):
        pltpu.make_async_copy(ref, ref, sem).wait()

    def dinv_send(l):
        row_send(lambda z: dinv.at[l, pl.ds(z * OWN, OWN)], lambda o: dv.at[l, o], sem_dv.at[0, l], sem_dv.at[1, l])
        pltpu.make_async_copy(dinv.at[l, pl.ds(row * OWN, OWN)], dv.at[l, row], sem_dv.at[2, l]).start()

    def dinv_wait(l):
        wait_bytes(dv.at[l, pl.ds(0, NR - 1)], sem_dv.at[0, l])
        wait_bytes(dv.at[l, pl.ds(0, NR - 1)], sem_dv.at[1, l])
        wait_bytes(dv.at[l, 0], sem_dv.at[2, l])
        for j in range(OWN):
            for z in range(NR):
                dh[l, j, 16 * z : 16 * z + 16, :] = store_matrix(dv[l, z, j])

    def r_send(l):
        rs[l, row] = rsend[l, row]
        row_send(lambda z: rsend.at[l, z], lambda o: rs.at[l, o], sem_r.at[0, l], sem_r.at[1, l])

    def r_wait(l):
        wait_bytes(rs.at[l, pl.ds(0, NR - 1)], sem_r.at[0, l])
        wait_bytes(rs.at[l, pl.ds(0, NR - 1)], sem_r.at[1, l])

    def col_send(src, dst, send_sem, recv_sem):
        @pl.loop(1, ncol)
        def _(k):
            c = lax.rem(col + k, ncol)
            pltpu.make_async_remote_copy(
                src_ref=src.at[pl.ds(c * cap, cap)], dst_ref=dst.at[pl.ds(col * cap, cap)],
                send_sem=send_sem, recv_sem=recv_sem,
                device_id={"col": c}, device_id_type=pl.DeviceIdType.MESH,
            ).start()
        dst[pl.ds(col * cap, cap)] = src[pl.ds(col * cap, cap)]

    def col_wait(dst, sem):
        wait_bytes(dst.at[pl.ds(0, SLOTS - cap)], sem)

    def fwd_pack_send(l, g):
        a, b = FWD_GROUPS[g]
        src, dst = fsend[g], frecv[g].at[l]

        @pl.loop(0, SLOTS, unroll=4)
        def _(s):
            k = tab[l, FSRC, s]
            if l == 0 or a == 7:
                src[s] = out[k, pl.ds(a, b - a)]
            else:
                src[s] = out[k, pl.ds(a, b - a)] + car[k, pl.ds(a, b - a)]
        col_send(src, dst, sem_fs.at[l, g], sem_fr.at[l, g])

    def fwd_collect(l, g):
        a, b = FWD_GROUPS[g]
        dst = frecv[g].at[l]
        col_wait(dst, sem_fr.at[l, g])
        col_wait(fsend[g], sem_fs.at[l, g])

        @pl.loop(0, SLOTS, unroll=4)
        def _(s):
            cum[s, pl.ds(0, b - a)] = dst[s] + cum[tab[l, PREV, s], pl.ds(0, b - a)]

        if g == 0:
            @pl.loop(0, SUP, unroll=4)
            def _(p):
                rsend[l + 1, p // OWN, p % OWN] = rhs[l + 1, p] - cum[tab[l, LAST, p], 0]
        else:
            @pl.loop(0, SUP, unroll=4)
            def _(p):
                car[p, pl.ds(a - 1, b - a)] = cum[tab[l, LAST, p], pl.ds(0, b - a)]

    def bwd_pack_send(l, g, source):
        src, dst = bsend[l][g], brecv[l][g]

        @pl.loop(0, SLOTS, unroll=4)
        def _(s):
            src[s] = source(tab[l, BSRC, s])
        col_send(src, dst, sem_bs.at[l, g], sem_br.at[l, g])

    def bwd_gather(l, g):
        a, b = BWD_GROUPS[l][g]
        dst = brecv[l][g]
        col_wait(dst, sem_br.at[l, g])
        col_wait(bsend[l][g], sem_bs.at[l, g])

        @pl.loop(0, SUP, unroll=4)
        def _(k):
            anct[l, k, pl.ds(a, b - a)] = dst[tab[l, POS, k]]

    def convert(l):
        load_panels(l).wait()

        @pl.loop(0, SUP)
        def _(g):
            for d in range(ANC):
                block = stage[l % 2, d, g]
                if d > 0:
                    block = block * pat[l, d - 1, g].astype(F32)
                ph[l, g, 16 * d : 16 * d + 16, :] = store_matrix(block)
        if l + 2 < LEVELS:
            load_panels(l + 2).start()

    def ag_copy(l, c, t, way):
        origin = at_row(1 - t) if way == 0 else at_row(t - 1)
        return pltpu.make_async_remote_copy(
            src_ref=sol.at[l, origin, c], dst_ref=sol.at[l, origin, c],
            send_sem=sem_ag_s.at[l, c, t - 1, way], recv_sem=sem_ag_r.at[l, c, t - 1, way],
            device_id=rowdev(right if way == 0 else left), device_id_type=pl.DeviceIdType.MESH,
        )

    def ag_ways(c, t):
        return (0, 1) if t < 4 else (c % 2,)

    def product(l, g):
        out[g] = apply(ph[l, g], expand(sol[l, g // OWN, g % OWN].reshape(8, 8, 128)))

    def solve(l):
        r_wait(l)
        for c in range(OWN):
            sol[l, row, c] = apply(dh[l, c], expand(rs[l, :, c])).reshape(64, 128)
            for way in ag_ways(c, 1):
                ag_copy(l, c, 1, way).start()

    def spread_solved(l):
        @pl.loop(0, OWN)
        def _(c):
            product(l, row * OWN + c)
        for t in range(1, 5):
            for c in range(OWN):
                for way in ag_ways(c, t):
                    ag_copy(l, c, t, way).wait_recv()
                    if t < 4 and way in ag_ways(c, t + 1):
                        ag_copy(l, c, t + 1, way).start()
                if t == 4:
                    product(l, at_row(4) * OWN + c)
                else:
                    @pl.loop(0, 2)
                    def _(w):
                        product(l, lax.rem(row + NR - t + 2 * t * w, NR) * OWN + c)
        for t in range(1, 5):
            for c in range(OWN):
                for way in ag_ways(c, t):
                    ag_copy(l, c, t, way).wait_send()

    def rs_dest(t, way):
        return at_row(5 - t) if way == 0 else at_row(t - 5)

    def rs_ways(c, t):
        return (0, 1) if t > 1 else (c % 2,)

    def rs_copy(l, c, t, way):
        first = t == 1 or way not in rs_ways(c, t - 1)
        src = part.at[rs_dest(t, way), c] if first else rsr.at[l, way, t - 2, c]
        return pltpu.make_async_remote_copy(
            src_ref=src, dst_ref=rsr.at[l, way, t - 1, c],
            send_sem=sem_rs_s.at[l, c, t - 1, way], recv_sem=sem_rs_r.at[l, c, t - 1, way],
            device_id=rowdev(right if way == 0 else left), device_id_type=pl.DeviceIdType.MESH,
        )

    def sum_over_row(l, make):
        for t in range(1, 5):
            if t == 1:
                for c in range(OWN):
                    make(at_row(4) * OWN + c)
            else:
                for c in range(OWN):
                    @pl.loop(0, 2)
                    def _(w):
                        make(lax.rem(row + NR + (5 - t) * (1 - 2 * w), NR) * OWN + c)
            for c in range(OWN):
                for way in rs_ways(c, t):
                    if t > 1 and way in rs_ways(c, t - 1):
                        rs_copy(l, c, t - 1, way).wait_recv()
                        rsr[l, way, t - 2, c] += part[rs_dest(t, way), c]
                    rs_copy(l, c, t, way).start()
        for c in range(OWN):
            make(row * OWN + c)
        for c in range(OWN):
            for way in (0, 1):
                rs_copy(l, c, 4, way).wait_recv()
            tot[l, c] = part[row, c] + rsr[l, 0, 3, c] + rsr[l, 1, 3, c]
        for c in range(OWN):
            for t in range(1, 5):
                for way in rs_ways(c, t):
                    rs_copy(l, c, t, way).wait_send()

    def finish(l):
        for c in range(OWN):
            reduced = (sol[l, row, c] - tot[l, c]).reshape(8, 8, 128)
            xsend[l, :, c] = apply_t(dh[l, c], reduced)
        solr[l, row] = xsend[l, row]
        row_send(lambda z: xsend.at[l, z], lambda o: solr.at[l, o], sem_x.at[0, l], sem_x.at[1, l])
        wait_bytes(solr.at[l, pl.ds(0, NR - 1)], sem_x.at[1, l])
        wait_bytes(solr.at[l, pl.ds(0, NR - 1)], sem_x.at[0, l])

    def emit(l):
        sol_out[l] = solr[l].reshape(SUP, 8, 128)

    def set_part(g, value):
        part[g // OWN, g % OWN] = value.reshape(64, 128)

    for l in range(LEVELS):
        dinv_send(l)
    rsend[0] = rhs[0].reshape(NR, OWN, 8, 128)
    r_send(0)
    cum[SLOTS] = jnp.zeros(cum.shape[1:], F32)
    bwd_pack_send(2, 1, lambda k: anc[k, pl.ds(0, 7)])
    convert(0)
    dinv_wait(0)
    for l in range(LEVELS - 1):
        solve(l)
        spread_solved(l)
        if l > 0:
            fwd_collect(l - 1, 1)
        fwd_pack_send(l, 0)
        if l > 0:
            fwd_collect(l - 1, 2)

            @pl.loop(0, SUP)
            def _(g):
                car[g, 7] = jnp.zeros((8, 128), F32)
        fwd_pack_send(l, 1)
        fwd_pack_send(l, 2)
        convert(l + 1)
        dinv_wait(l + 1)
        if l == 0:
            bwd_gather(2, 1)
            bwd_pack_send(1, 2, lambda k: anct[2, k, pl.ds(1, 6)])
        if l == 1:
            bwd_gather(1, 2)
            bwd_pack_send(0, 3, lambda k: anct[1, k, pl.ds(2, 5)])
        if l == 2:
            sum_over_row(3, lambda g: set_part(g, apply_t(ph[3, g], anc[g])))
        fwd_collect(l, 0)
        r_send(l + 1)

    solve(3)
    finish(3)
    bwd_pack_send(2, 0, lambda k: solr[3, k // OWN, pl.ds(k % OWN, 1)])
    emit(3)
    spread_solved(3)
    fwd_collect(2, 1)
    fwd_collect(2, 2)

    @pl.loop(0, SUP)
    def _(g):
        bu_out[g, pl.ds(0, 7)] = out[g, pl.ds(0, 7)] + car[g, pl.ds(0, 7)]
        bu_out[g, 7] = out[g, 7]

    for l in (2, 1, 0):
        if l == 1:
            bwd_gather(1, 1)
        if l == 0:
            bwd_gather(0, 3)
            bwd_gather(0, 2)
            bwd_gather(0, 1)

        @pl.loop(0, SUP)
        def _(g):
            set_part(g, apply_t(ph[l, g, 16:, :], anct[l, g, pl.ds(1, 7)]))
        bwd_gather(l, 0)
        if l == 2:
            bwd_pack_send(1, 1, lambda k: anct[2, k, pl.ds(0, 1)])
        if l == 1:
            bwd_pack_send(0, 1, lambda k: anct[1, k, pl.ds(0, 1)])
            bwd_pack_send(0, 2, lambda k: anct[1, k, pl.ds(1, 1)])

        def add_part(g):
            extra = apply_t(ph[l, g, 0:16, :], anct[l, g, pl.ds(0, 1)])
            part[g // OWN, g % OWN] += extra.reshape(64, 128)
        sum_over_row(l, add_part)
        finish(l)
        if l > 0:
            bwd_pack_send(l - 1, 0, lambda k: solr[l, k // OWN, pl.ds(k % OWN, 1)])
        emit(l)


def tables(parent_owner, parent_local, ncol):
    cap = SLOTS // ncol
    owner = parent_owner[:, :, 0]
    here = jnp.arange(SUP, dtype=jnp.int32)
    same = (owner[:, :, None] == owner[:, None, :]) & (here[None, :, None] < here[None, None, :])
    pos = owner * cap + jnp.sum(same.astype(jnp.int32), axis=1)
    slots = jnp.arange(SLOTS, dtype=jnp.int32)
    hit = pos[:, None, :] == slots[None, :, None]
    fsrc = jnp.sum(jnp.where(hit, here[None, None, :], 0), axis=2)
    ids = jnp.sum(jnp.where(hit, parent_local[:, None, :] + 1, 0), axis=2)
    ids = lax.all_to_all(ids.reshape(3, ncol, cap), "col", split_axis=1, concat_axis=1, tiled=True).reshape(3, SLOTS)
    equal = (ids[:, :, None] == ids[:, None, :]) & (slots[None, None, :] < slots[None, :, None])
    prev = jnp.max(jnp.where(equal, slots[None, None, :], -1), axis=2)
    prev = jnp.where(prev < 0, SLOTS, prev)
    mine = ids[:, None, :] == here[None, :, None] + 1
    last = jnp.max(jnp.where(mine, slots[None, None, :], -1), axis=2)
    last = jnp.where(last < 0, SLOTS, last)
    bsrc = jnp.maximum(ids - 1, 0)
    wide = lambda x: jnp.pad(x, ((0, 0), (0, SLOTS - x.shape[1])))
    return jnp.stack([fsrc, wide(pos), prev, wide(last), bsrc], axis=1)


def per_device(ncol, rhs, dinv, panels, pattern, parent_owner, parent_local, ancestor_solution):
    tab = tables(parent_owner, parent_local, ncol)
    rhs_p = rhs.reshape(LEVELS, 2, 8, SUP, 64).transpose(0, 3, 2, 1, 4).reshape(LEVELS, SUP, 8, 128)
    anc_p = ancestor_solution.reshape(2, 8, SUP, ANC, 64).transpose(2, 3, 1, 0, 4).reshape(SUP, ANC, 8, 128)
    vmem = pl.BlockSpec(memory_space=pltpu.VMEM)
    smem = pl.BlockSpec(memory_space=pltpu.SMEM)
    anywhere = pl.BlockSpec(memory_space=pl.ANY)
    sems = pltpu.SemaphoreType.DMA
    tile = (8, 128)
    fsend = tuple(pltpu.VMEM((SLOTS, b - a) + tile, F32) for a, b in FWD_GROUPS)
    frecv = tuple(pltpu.VMEM((3, SLOTS, b - a) + tile, F32) for a, b in FWD_GROUPS)
    bbuf = tuple(tuple(pltpu.VMEM((SLOTS, b - a) + tile, F32) for a, b in groups) for groups in BWD_GROUPS)
    sol, bu = pl.pallas_call(
        functools.partial(kernel, ncol),
        out_shape=(
            jax.ShapeDtypeStruct((LEVELS, SUP) + tile, F32),
            jax.ShapeDtypeStruct((SUP, ANC) + tile, F32),
        ),
        in_specs=[smem, smem, vmem, vmem, anywhere, anywhere],
        out_specs=(vmem, vmem),
        scratch_shapes=[
            pltpu.VMEM((2, ANC, SUP, 16, 128), F32),
            pltpu.VMEM((LEVELS, SUP, 128, 256), BF16),
            pltpu.VMEM((LEVELS, NR, OWN, 16, 128), F32),
            pltpu.VMEM((LEVELS, OWN, 128, 256), BF16),
            pltpu.VMEM((LEVELS, NR, OWN) + tile, F32),
            pltpu.VMEM((LEVELS, NR, OWN) + tile, F32),
            pltpu.VMEM((LEVELS, NR, OWN, 64, 128), F32),
            pltpu.VMEM((SUP, ANC) + tile, F32),
            pltpu.VMEM((SUP, ANC) + tile, F32),
            pltpu.VMEM((SLOTS + 1, 6) + tile, F32),
            fsend, frecv, bbuf, bbuf,
            pltpu.VMEM((3, SUP, ANC) + tile, F32),
            pltpu.VMEM((NR, OWN, 64, 128), F32),
            pltpu.VMEM((LEVELS, 2, 4, OWN, 64, 128), F32),
            pltpu.VMEM((LEVELS, OWN, 64, 128), F32),
            pltpu.VMEM((LEVELS, NR, OWN) + tile, F32),
            pltpu.VMEM((LEVELS, NR, OWN) + tile, F32),
            sems((2,)), sems((3, LEVELS)), sems((2, LEVELS)),
            sems((LEVELS, OWN, 4, 2)), sems((LEVELS, OWN, 4, 2)),
            sems((3, 3)), sems((3, 3)), sems((3, 4)), sems((3, 4)),
            sems((LEVELS, OWN, 4, 2)), sems((LEVELS, OWN, 4, 2)), sems((2, LEVELS)),
        ],
        compiler_params=pltpu.CompilerParams(
            collective_id=0, has_side_effects=True, vmem_limit_bytes=60 * 1024 * 1024
        ),
        cost_estimate=pl.CostEstimate(flops=4 * 10**9, bytes_accessed=12 * 10**6, transcendentals=0),
    )(tab, pattern, rhs_p, anc_p, dinv, panels)
    solution = sol.reshape(LEVELS, SUP, 8, 2, 64).transpose(0, 3, 2, 1, 4).reshape(LEVELS, 16, SUP, 64)
    boundary = bu.reshape(SUP, ANC, 8, 2, 64).transpose(3, 2, 0, 1, 4).reshape(16, SUP, ANC, 64)
    return solution, boundary


def solution(mesh):
    placed = (
        P(None, "row", "col", None),
        P(None, "col", "row", None),
        P(None, None, "col", "row", None),
        P(None, None, "col"),
        P(None, "col", None),
        P(None, "col"),
        P("row", "col", None, None),
    )
    return jax.shard_map(
        functools.partial(per_device, mesh.shape["col"]),
        mesh=mesh,
        in_specs=placed,
        out_specs=(P(None, "row", "col", None), P("row", "col", None, None)),
        check_vma=False,
    )
```

```python
import functools

import jax
import jax.numpy as jnp
from jax import lax
from jax.experimental import pallas as pl
from jax.experimental.pallas import tpu as pltpu
from jax.sharding import PartitionSpec as P

F32 = jnp.float32
BF16 = jnp.bfloat16
LEVELS = 4
ANC = 8
SUP = 32
SLOTS = 64
NR = 8
OWN = SUP // NR
FWD_GROUPS = ((0, 1), (1, 2), (2, 8))
BWD_GROUPS = (((0, 1), (1, 2), (2, 3), (3, 8)), ((0, 1), (1, 2), (2, 8)), ((0, 1), (1, 8)))
FSRC, POS, PREV, LAST, BSRC = range(5)


def low_lanes(shape):
    return lax.broadcasted_iota(jnp.int32, shape, len(shape) - 1) < 64


def swap_halves(x):
    return pltpu.roll(x.reshape(-1, 128), 64, 1).reshape(x.shape)


def split(x):
    high = x.astype(BF16).astype(F32)
    return high, x - high


def store_matrix(block):
    high, low = split(block)
    return jnp.concatenate([high.astype(BF16), low.astype(BF16)], axis=1)


def multiply(matrix, tiles):
    low = low_lanes((8, 128))
    high, rest = split(tiles)
    high_r, rest_r = swap_halves(high), swap_halves(rest)
    rows = []
    for z in range(8):
        rows += [jnp.where(low, high[z], rest_r[z]), jnp.where(low, high_r[z], rest[z])]
    weights = jnp.concatenate(rows, axis=0).astype(BF16)
    weights = jnp.concatenate([weights, weights], axis=0)
    o = jnp.dot(matrix, weights, preferred_element_type=F32).reshape(8, 2, 8, 128)
    low = low_lanes((8, 8, 128))
    return jnp.where(low, o[:, 0], o[:, 1]) + swap_halves(jnp.where(low, o[:, 1], o[:, 0]))


def kernel(
    ncol, tab, pat, rhs, anc, dinv, panels, sol_out, bu_out,
    stage, ph, pt, dv, dh, dt, rsend, rs, sol, out, car, cum, fsend, frecv, bsend, bulk, brecv, anct,
    part, rsr, tot, xsend, solr,
    sem_stage, sem_dv, sem_r, sem_ag_s, sem_ag_r, sem_fs, sem_fr, sem_bs, sem_br, sem_rs_s, sem_rs_r, sem_x,
):
    row, col = lax.axis_index("row"), lax.axis_index("col")
    cap = SLOTS // ncol
    right, left = lax.rem(row + 1, NR), lax.rem(row + NR - 1, NR)

    def rowdev(z):
        return {"row": z}

    def at_row(offset):
        return lax.rem(row + offset + 2 * NR, NR)

    barrier = pltpu.get_barrier_semaphore()

    @pl.loop(1, NR)
    def _(k):
        pl.semaphore_signal(barrier, inc=1, device_id=rowdev(lax.rem(row + k, NR)), device_id_type=pl.DeviceIdType.MESH)

    @pl.loop(1, ncol)
    def _(k):
        pl.semaphore_signal(barrier, inc=1, device_id={"col": lax.rem(col + k, ncol)}, device_id_type=pl.DeviceIdType.MESH)

    def load_panels(l):
        place = (0, 0, 1, 1)[l]
        return pltpu.make_async_copy(panels.at[l], stage.at[place], sem_stage.at[place])

    load_panels(0).start()
    load_panels(3).start()
    pl.semaphore_wait(barrier, NR - 1 + ncol - 1)

    def row_send(src, dst, send_sem, recv_sem):
        for k in (4, 3, 5, 2, 6, 1, 7):
            z = lax.rem(row + k, NR)
            pltpu.make_async_remote_copy(
                src_ref=src(z), dst_ref=dst(row), send_sem=send_sem, recv_sem=recv_sem,
                device_id=rowdev(z), device_id_type=pl.DeviceIdType.MESH,
            ).start()

    def wait_bytes(ref, sem):
        pltpu.make_async_copy(ref, ref, sem).wait()

    def dinv_send(l):
        row_send(lambda z: dinv.at[l, pl.ds(z * OWN, OWN)], lambda o: dv.at[l, o], sem_dv.at[0, l], sem_dv.at[1, l])
        pltpu.make_async_copy(dinv.at[l, pl.ds(row * OWN, OWN)], dv.at[l, row], sem_dv.at[2, l]).start()

    def dinv_wait(l):
        wait_bytes(dv.at[l, pl.ds(0, NR - 1)], sem_dv.at[0, l])
        wait_bytes(dv.at[l, pl.ds(0, NR - 1)], sem_dv.at[1, l])
        wait_bytes(dv.at[l, 0], sem_dv.at[2, l])
        for j in range(OWN):
            whole = dv[l, :, j].reshape(128, 128)
            dh[l, j] = store_matrix(whole)
            dt[l, j] = store_matrix(whole.T)

    def r_send(l):
        rs[l, row] = rsend[l, row]
        for h in range(2):
            part_h = pl.ds(2 * h, 2)
            row_send(
                lambda z: rsend.at[l, z, part_h], lambda o: rs.at[l, o, part_h], sem_r.at[0, l, h], sem_r.at[1, l, h]
            )

    def r_wait(l, h):
        wait_bytes(rs.at[l, pl.ds(0, NR - 1), pl.ds(2 * h, 2)], sem_r.at[1, l, h])

    def r_wait_sent(l):
        for h in range(2):
            wait_bytes(rs.at[l, pl.ds(0, NR - 1), pl.ds(2 * h, 2)], sem_r.at[0, l, h])

    def col_send(src, dst, send_sem, recv_sem):
        @pl.loop(1, ncol)
        def _(k):
            c = lax.rem(col + k, ncol)
            pltpu.make_async_remote_copy(
                src_ref=src.at[pl.ds(c * cap, cap)], dst_ref=dst.at[pl.ds(col * cap, cap)],
                send_sem=send_sem, recv_sem=recv_sem,
                device_id={"col": c}, device_id_type=pl.DeviceIdType.MESH,
            ).start()
        dst[pl.ds(col * cap, cap)] = src[pl.ds(col * cap, cap)]

    def col_wait(dst, sem):
        wait_bytes(dst.at[pl.ds(0, SLOTS - cap)], sem)

    def fwd_pack_send(l, g):
        a, b = FWD_GROUPS[g]
        src, dst = fsend[g], frecv[g].at[l % 2]

        @pl.loop(0, SLOTS, unroll=4)
        def _(s):
            k = tab[l, FSRC, s]
            if l == 0 or a == 7:
                src[s] = out[k, pl.ds(a, b - a)]
            else:
                src[s] = out[k, pl.ds(a, b - a)] + car[k, pl.ds(a, b - a)]
        col_send(src, dst, sem_fs.at[l, g], sem_fr.at[l, g])

    def fwd_collect(l, g):
        a, b = FWD_GROUPS[g]
        dst = frecv[g].at[l % 2]
        col_wait(dst, sem_fr.at[l, g])
        col_wait(fsend[g], sem_fs.at[l, g])

        @pl.loop(0, SLOTS, unroll=4)
        def _(s):
            cum[s, pl.ds(0, b - a)] = dst[s] + cum[tab[l, PREV, s], pl.ds(0, b - a)]

        if g == 0:
            @pl.loop(0, SUP, unroll=4)
            def _(p):
                rsend[l + 1, p // OWN, p % OWN] = rhs[l + 1, p] - cum[tab[l, LAST, p], 0]
        else:
            @pl.loop(0, SUP, unroll=4)
            def _(p):
                car[p, pl.ds(a - 1, b - a)] = cum[tab[l, LAST, p], pl.ds(0, b - a)]

    def bwd_buffer(l, g):
        a, b = BWD_GROUPS[l][g]
        return bulk.at[:, pl.ds(0, b - a)] if b - a > 1 else bsend.at[l, g]

    def bwd_pack_send(l, g, source):
        src, dst = bwd_buffer(l, g), brecv[l][g]

        @pl.loop(0, SLOTS, unroll=4)
        def _(s):
            src[s] = source(tab[l, BSRC, s])
        col_send(src, dst, sem_bs.at[l, g], sem_br.at[l, g])

    def bwd_gather(l, g):
        a, b = BWD_GROUPS[l][g]
        dst = brecv[l][g]
        col_wait(dst, sem_br.at[l, g])
        col_wait(bwd_buffer(l, g), sem_bs.at[l, g])

        @pl.loop(0, SUP, unroll=4)
        def _(k):
            anct[l, k, pl.ds(a, b - a)] = dst[tab[l, POS, k]]

    def convert(l):
        load_panels(l).wait()

        @pl.loop(0, SUP)
        def _(g):
            blocks = [stage[(0, 0, 1, 1)[l], 0, g]]
            for d in range(1, ANC):
                blocks.append(stage[(0, 0, 1, 1)[l], d, g] * pat[l, d - 1, g].astype(F32))
            whole = jnp.concatenate(blocks, axis=0)
            ph[l, g] = store_matrix(whole)
            pt[l, g] = store_matrix(whole.T)
        if l in (0, 3):
            load_panels((1, None, None, 2)[l]).start()

    def ag_copy(l, c, t, way):
        origin = at_row(1 - t) if way == 0 else at_row(t - 1)
        return pltpu.make_async_remote_copy(
            src_ref=sol.at[l, origin, c], dst_ref=sol.at[l, origin, c],
            send_sem=sem_ag_s.at[l, c, t - 1, way], recv_sem=sem_ag_r.at[l, c, t - 1, way],
            device_id=rowdev(right if way == 0 else left), device_id_type=pl.DeviceIdType.MESH,
        )

    def ag_ways(c, t):
        return (0, 1) if t < 4 else (c % 2,)

    def product(l, g):
        out[g] = multiply(ph[l, g], sol[l, g // OWN, g % OWN].reshape(8, 8, 128))

    def solve(l):
        for c in range(OWN):
            if c % 2 == 0:
                r_wait(l, c // 2)
            sol[l, row, c] = multiply(dh[l, c], rs[l, :, c]).reshape(64, 128)
            for way in ag_ways(c, 1):
                ag_copy(l, c, 1, way).start()
        r_wait_sent(l)

    def spread_solved(l, extra=None):
        for c in range(OWN):
            product(l, row * OWN + c)
        for t in range(1, 5):
            for c in range(OWN):
                for way in ag_ways(c, t):
                    ag_copy(l, c, t, way).wait_recv()
                    if t < 4 and way in ag_ways(c, t + 1):
                        ag_copy(l, c, t + 1, way).start()
                if t == 4:
                    product(l, at_row(4) * OWN + c)
                else:
                    for offset in (-t, t):
                        product(l, at_row(offset) * OWN + c)
            if extra is not None:
                extra(t)
        for t in range(1, 5):
            for c in range(OWN):
                for way in ag_ways(c, t):
                    ag_copy(l, c, t, way).wait_send()

    def rs_dest(t, way):
        return at_row(5 - t) if way == 0 else at_row(t - 5)

    def rs_ways(c, t):
        return (0, 1) if t > 1 else (c % 2,)

    def rs_copy(l, c, t, way):
        first = t == 1 or way not in rs_ways(c, t - 1)
        src = part.at[rs_dest(t, way), c] if first else rsr.at[l % 2, way, t - 2, c]
        return pltpu.make_async_remote_copy(
            src_ref=src, dst_ref=rsr.at[l % 2, way, t - 1, c],
            send_sem=sem_rs_s.at[l, c, t - 1, way], recv_sem=sem_rs_r.at[l, c, t - 1, way],
            device_id=rowdev(right if way == 0 else left), device_id_type=pl.DeviceIdType.MESH,
        )

    def ring_step(l, t):
        for c in range(OWN):
            for way in rs_ways(c, t):
                if t > 1 and way in rs_ways(c, t - 1):
                    rs_copy(l, c, t - 1, way).wait_recv()
                    rsr[l % 2, way, t - 2, c] += part[rs_dest(t, way), c]
                rs_copy(l, c, t, way).start()

    def ring_end(l, done):
        for c in range(OWN):
            for way in (0, 1):
                rs_copy(l, c, 4, way).wait_recv()
            total = part[row, c] + rsr[l % 2, 0, 3, c] + rsr[l % 2, 1, 3, c]
            done(c, total)
        for c in range(OWN):
            for t in range(1, 5):
                for way in rs_ways(c, t):
                    rs_copy(l, c, t, way).wait_send()

    def sum_over_row(l, make, done):
        for t in range(1, 5):
            for offset in (4,) if t == 1 else (5 - t, t - 5):
                for c in range(OWN):
                    make(at_row(offset) * OWN + c)
            ring_step(l, t)
        for c in range(OWN):
            make(row * OWN + c)
        ring_end(l, done)

    def keep(c, total):
        tot[c] = total

    def finish(l, c, total):
        reduced = (sol[l, row, c] - total).reshape(8, 8, 128)
        xsend[l, :, c] = multiply(dt[l, c], reduced)
        if c % 2 == 1:
            h = c // 2
            part_h = pl.ds(2 * h, 2)
            solr[l, row, part_h] = xsend[l, row, part_h]
            row_send(
                lambda z: xsend.at[l, z, part_h], lambda o: solr.at[l, o, part_h], sem_x.at[0, l, h], sem_x.at[1, l, h]
            )

    def finish_wait(l):
        for h in range(2):
            for k in (1, 0):
                wait_bytes(solr.at[l, pl.ds(0, NR - 1), pl.ds(2 * h, 2)], sem_x.at[k, l, h])

    def emit(l):
        sol_out[l] = solr[l].reshape(SUP, 8, 128)

    def set_part(g, value):
        part[g // OWN, g % OWN] = value.reshape(64, 128)

    def top_part(t):
        @pl.loop(8 * t - 8, 8 * t, unroll=2)
        def _(g):
            set_part(g, multiply(pt[3, g], anc[g]))

    rsend[0] = rhs[0].reshape(NR, OWN, 8, 128)
    r_send(0)
    dinv_send(0)
    cum[SLOTS] = jnp.zeros(cum.shape[1:], F32)
    bwd_pack_send(2, 1, lambda k: anc[k, pl.ds(0, 7)])
    convert(0)
    convert(3)
    dinv_wait(0)
    for l in range(LEVELS - 1):
        solve(l)
        spread_solved(l, top_part if l == 0 else None)
        if l > 0:
            fwd_collect(l - 1, 1)
        fwd_pack_send(l, 0)
        dinv_send(l + 1)
        ring_step(3, (1, 3, 4)[l])
        if l > 0:
            fwd_collect(l - 1, 2)

            @pl.loop(0, SUP)
            def _(g):
                car[g, 7] = jnp.zeros((8, 128), F32)
        fwd_pack_send(l, 1)
        fwd_pack_send(l, 2)
        if l + 1 < 3:
            convert(l + 1)
        if l == 0:
            ring_step(3, 2)
        fwd_collect(l, 0)
        r_send(l + 1)
        dinv_wait(l + 1)
        if l == 0:
            bwd_gather(2, 1)
            bwd_pack_send(1, 2, lambda k: anct[2, k, pl.ds(1, 6)])
        if l == 1:
            bwd_gather(1, 2)
            bwd_pack_send(0, 3, lambda k: anct[1, k, pl.ds(2, 5)])

    ring_end(3, keep)
    solve(3)
    for c in range(OWN):
        finish(3, c, tot[c])
    finish_wait(3)
    bwd_pack_send(2, 0, lambda k: solr[3, k // OWN, pl.ds(k % OWN, 1)])
    emit(3)
    spread_solved(3)
    fwd_collect(2, 1)
    fwd_collect(2, 2)

    @pl.loop(0, SUP)
    def _(g):
        bu_out[g, pl.ds(0, 7)] = out[g, pl.ds(0, 7)] + car[g, pl.ds(0, 7)]
        bu_out[g, 7] = out[g, 7]

    for l in (2, 1, 0):
        if l == 1:
            bwd_gather(1, 1)
        if l == 0:
            bwd_gather(0, 3)
            bwd_gather(0, 2)
            bwd_gather(0, 1)
        bwd_gather(l, 0)
        if l == 2:
            bwd_pack_send(1, 1, lambda k: anct[2, k, pl.ds(0, 1)])
        if l == 1:
            bwd_pack_send(0, 1, lambda k: anct[1, k, pl.ds(0, 1)])
            bwd_pack_send(0, 2, lambda k: anct[1, k, pl.ds(1, 1)])

        sum_over_row(
            l, lambda g: set_part(g, multiply(pt[l, g], anct[l, g])), functools.partial(finish, l)
        )
        finish_wait(l)
        if l > 0:
            bwd_pack_send(l - 1, 0, lambda k: solr[l, k // OWN, pl.ds(k % OWN, 1)])
        emit(l)


def tables(parent_owner, parent_local, ncol):
    cap = SLOTS // ncol
    owner = parent_owner[:, :, 0]
    here = jnp.arange(SUP, dtype=jnp.int32)
    same = (owner[:, :, None] == owner[:, None, :]) & (here[None, :, None] < here[None, None, :])
    pos = owner * cap + jnp.sum(same.astype(jnp.int32), axis=1)
    slots = jnp.arange(SLOTS, dtype=jnp.int32)
    hit = pos[:, None, :] == slots[None, :, None]
    fsrc = jnp.sum(jnp.where(hit, here[None, None, :], 0), axis=2)
    ids = jnp.sum(jnp.where(hit, parent_local[:, None, :] + 1, 0), axis=2)
    ids = lax.all_to_all(ids.reshape(3, ncol, cap), "col", split_axis=1, concat_axis=1, tiled=True).reshape(3, SLOTS)
    equal = (ids[:, :, None] == ids[:, None, :]) & (slots[None, None, :] < slots[None, :, None])
    prev = jnp.max(jnp.where(equal, slots[None, None, :], -1), axis=2)
    prev = jnp.where(prev < 0, SLOTS, prev)
    mine = ids[:, None, :] == here[None, :, None] + 1
    last = jnp.max(jnp.where(mine, slots[None, None, :], -1), axis=2)
    last = jnp.where(last < 0, SLOTS, last)
    bsrc = jnp.maximum(ids - 1, 0)
    wide = lambda x: jnp.pad(x, ((0, 0), (0, SLOTS - x.shape[1])))
    return jnp.stack([fsrc, wide(pos), prev, wide(last), bsrc], axis=1)


def per_device(ncol, rhs, dinv, panels, pattern, parent_owner, parent_local, ancestor_solution):
    tab = tables(parent_owner, parent_local, ncol)
    rhs_p = rhs.reshape(LEVELS, 2, 8, SUP, 64).transpose(0, 3, 2, 1, 4).reshape(LEVELS, SUP, 8, 128)
    anc_p = ancestor_solution.reshape(2, 8, SUP, ANC, 64).transpose(2, 3, 1, 0, 4).reshape(SUP, ANC, 8, 128)
    vmem = pl.BlockSpec(memory_space=pltpu.VMEM)
    smem = pl.BlockSpec(memory_space=pltpu.SMEM)
    anywhere = pl.BlockSpec(memory_space=pl.ANY)
    sems = pltpu.SemaphoreType.DMA
    tile = (8, 128)
    fsend = tuple(pltpu.VMEM((SLOTS, b - a) + tile, F32) for a, b in FWD_GROUPS)
    frecv = tuple(pltpu.VMEM((2, SLOTS, b - a) + tile, F32) for a, b in FWD_GROUPS)
    bbuf = tuple(tuple(pltpu.VMEM((SLOTS, b - a) + tile, F32) for a, b in groups) for groups in BWD_GROUPS)
    sol, bu = pl.pallas_call(
        functools.partial(kernel, ncol),
        out_shape=(
            jax.ShapeDtypeStruct((LEVELS, SUP) + tile, F32),
            jax.ShapeDtypeStruct((SUP, ANC) + tile, F32),
        ),
        in_specs=[smem, smem, vmem, vmem, anywhere, anywhere],
        out_specs=(vmem, vmem),
        scratch_shapes=[
            pltpu.VMEM((2, ANC, SUP, 16, 128), F32),
            pltpu.VMEM((LEVELS, SUP, 128, 256), BF16),
            pltpu.VMEM((LEVELS, SUP, 128, 256), BF16),
            pltpu.VMEM((LEVELS, NR, OWN, 16, 128), F32),
            pltpu.VMEM((LEVELS, OWN, 128, 256), BF16),
            pltpu.VMEM((LEVELS, OWN, 128, 256), BF16),
            pltpu.VMEM((LEVELS, NR, OWN) + tile, F32),
            pltpu.VMEM((LEVELS, NR, OWN) + tile, F32),
            pltpu.VMEM((LEVELS, NR, OWN, 64, 128), F32),
            pltpu.VMEM((SUP, ANC) + tile, F32),
            pltpu.VMEM((SUP, ANC) + tile, F32),
            pltpu.VMEM((SLOTS + 1, 6) + tile, F32),
            fsend, frecv, pltpu.VMEM((3, 3, SLOTS, 1) + tile, F32), pltpu.VMEM((SLOTS, 7) + tile, F32), bbuf,
            pltpu.VMEM((3, SUP, ANC) + tile, F32),
            pltpu.VMEM((NR, OWN, 64, 128), F32),
            pltpu.VMEM((2, 2, 4, OWN, 64, 128), F32),
            pltpu.VMEM((OWN, 64, 128), F32),
            pltpu.VMEM((LEVELS, NR, OWN) + tile, F32),
            pltpu.VMEM((LEVELS, NR, OWN) + tile, F32),
            sems((2,)), sems((3, LEVELS)), sems((2, LEVELS, 2)),
            sems((LEVELS, OWN, 4, 2)), sems((LEVELS, OWN, 4, 2)),
            sems((3, 3)), sems((3, 3)), sems((3, 4)), sems((3, 4)),
            sems((LEVELS, OWN, 4, 2)), sems((LEVELS, OWN, 4, 2)), sems((2, LEVELS, 2)),
        ],
        compiler_params=pltpu.CompilerParams(
            collective_id=0, has_side_effects=True, vmem_limit_bytes=60 * 1024 * 1024
        ),
        cost_estimate=pl.CostEstimate(flops=4 * 10**9, bytes_accessed=12 * 10**6, transcendentals=0),
    )(tab, pattern, rhs_p, anc_p, dinv, panels)
    solution = sol.reshape(LEVELS, SUP, 8, 2, 64).transpose(0, 3, 2, 1, 4).reshape(LEVELS, 16, SUP, 64)
    boundary = bu.reshape(SUP, ANC, 8, 2, 64).transpose(3, 2, 0, 1, 4).reshape(16, SUP, ANC, 64)
    return solution, boundary


def solution(mesh):
    placed = (
        P(None, "row", "col", None),
        P(None, "col", "row", None),
        P(None, None, "col", "row", None),
        P(None, None, "col"),
        P(None, "col", None),
        P(None, "col"),
        P("row", "col", None, None),
    )
    return jax.shard_map(
        functools.partial(per_device, mesh.shape["col"]),
        mesh=mesh,
        in_specs=placed,
        out_specs=(P(None, "row", "col", None), P("row", "col", None, None)),
        check_vma=False,
    )
```

```python
import functools

import jax
import jax.numpy as jnp
from jax import lax
from jax.experimental import pallas as pl
from jax.experimental.pallas import tpu as pltpu
from jax.sharding import PartitionSpec as P

F32 = jnp.float32
BF16 = jnp.bfloat16
LEVELS = 4
ANC = 8
SUP = 32
SLOTS = 64
NR = 8
OWN = SUP // NR
FWD_GROUPS = ((0, 1), (1, 2), (2, 8))
BWD_GROUPS = (((0, 1), (1, 2), (2, 3), (3, 8)), ((0, 1), (1, 2), (2, 8)), ((0, 1), (1, 8)))
FSRC, POS, PREV, LAST, BSRC = range(5)


def low_lanes(shape):
    return lax.broadcasted_iota(jnp.int32, shape, len(shape) - 1) < 64


def swap_halves(x):
    return pltpu.roll(x.reshape(-1, 128), 64, 1).reshape(x.shape)


def split(x):
    high = x.astype(BF16).astype(F32)
    return high, x - high


def store_matrix(block):
    high, low = split(block)
    return jnp.concatenate([high.astype(BF16), low.astype(BF16)], axis=1)


def multiply(matrix, tiles):
    low = low_lanes((8, 128))
    high, rest = split(tiles)
    high_r, rest_r = swap_halves(high), swap_halves(rest)
    rows = []
    for z in range(8):
        rows += [jnp.where(low, high[z], rest_r[z]), jnp.where(low, high_r[z], rest[z])]
    weights = jnp.concatenate(rows, axis=0).astype(BF16)
    weights = jnp.concatenate([weights, weights], axis=0)
    o = jnp.dot(matrix, weights, preferred_element_type=F32).reshape(8, 2, 8, 128)
    low = low_lanes((8, 8, 128))
    return jnp.where(low, o[:, 0], o[:, 1]) + swap_halves(jnp.where(low, o[:, 1], o[:, 0]))


def kernel(
    ncol, tab, pat, rhs, anc, dinv, panels, sol_out, bu_out,
    stage, ph, pt, dv, dh, dt, pv, p0, rsend, rs, asend, ar, own, sol, out, car, cum, fsend, frecv, bsend, bulk, brecv, anct,
    part, rsr, tot, xsend, solr,
    sem_stage, sem_dv, sem_p, sem_a, sem_r, sem_ag_s, sem_ag_r, sem_fs, sem_fr, sem_bs, sem_br, sem_rs_s, sem_rs_r, sem_x,
):
    row, col = lax.axis_index("row"), lax.axis_index("col")
    cap = SLOTS // ncol
    right, left = lax.rem(row + 1, NR), lax.rem(row + NR - 1, NR)

    def rowdev(z):
        return {"row": z}

    def at_row(offset):
        return lax.rem(row + offset + 2 * NR, NR)

    barrier = pltpu.get_barrier_semaphore()

    @pl.loop(1, NR)
    def _(k):
        pl.semaphore_signal(barrier, inc=1, device_id=rowdev(lax.rem(row + k, NR)), device_id_type=pl.DeviceIdType.MESH)

    @pl.loop(1, ncol)
    def _(k):
        pl.semaphore_signal(barrier, inc=1, device_id={"col": lax.rem(col + k, ncol)}, device_id_type=pl.DeviceIdType.MESH)

    def load_panels(l):
        place = (0, 0, 1, 1)[l]
        return pltpu.make_async_copy(panels.at[l], stage.at[place], sem_stage.at[place])

    load_panels(0).start()
    load_panels(3).start()
    pl.semaphore_wait(barrier, NR - 1 + ncol - 1)

    def row_send(src, dst, send_sem, recv_sem):
        for k in (4, 3, 5, 2, 6, 1, 7):
            z = lax.rem(row + k, NR)
            pltpu.make_async_remote_copy(
                src_ref=src(z), dst_ref=dst(row), send_sem=send_sem, recv_sem=recv_sem,
                device_id=rowdev(z), device_id_type=pl.DeviceIdType.MESH,
            ).start()

    def wait_bytes(ref, sem):
        pltpu.make_async_copy(ref, ref, sem).wait()

    def dinv_send(l):
        row_send(lambda z: dinv.at[l, pl.ds(z * OWN, OWN)], lambda o: dv.at[l, o], sem_dv.at[0, l], sem_dv.at[1, l])
        pltpu.make_async_copy(dinv.at[l, pl.ds(row * OWN, OWN)], dv.at[l, row], sem_dv.at[2, l]).start()

    def dinv_wait(l):
        wait_bytes(dv.at[l, pl.ds(0, NR - 1)], sem_dv.at[0, l])
        wait_bytes(dv.at[l, pl.ds(0, NR - 1)], sem_dv.at[1, l])
        wait_bytes(dv.at[l, 0], sem_dv.at[2, l])
        for j in range(OWN):
            whole = dv[l, :, j].reshape(128, 128)
            dh[l, j] = store_matrix(whole)
            dt[l, j] = store_matrix(whole.T)

    def p0_send(l):
        row_send(lambda z: panels.at[l, 0, pl.ds(z * OWN, OWN)], lambda o: pv.at[l, o], sem_p.at[0, l], sem_p.at[1, l])
        pltpu.make_async_copy(panels.at[l, 0, pl.ds(row * OWN, OWN)], pv.at[l, row], sem_p.at[2, l]).start()

    def p0_wait(l):
        wait_bytes(pv.at[l, pl.ds(0, NR - 1)], sem_p.at[0, l])
        wait_bytes(pv.at[l, pl.ds(0, NR - 1)], sem_p.at[1, l])
        wait_bytes(pv.at[l, 0], sem_p.at[2, l])
        for j in range(OWN):
            p0[l, j] = store_matrix(pv[l, :, j].reshape(128, 128).T)

    def a_send(l):
        col_wait(brecv[l][0], sem_br.at[l, 0])
        col_wait(bwd_buffer(l, 0), sem_bs.at[l, 0])

        @pl.loop(0, SUP, unroll=4)
        def _(k):
            asend[l, k // OWN, k % OWN] = brecv[l][0][tab[l, POS, k], 0]
        ar[l, row] = asend[l, row]
        row_send(lambda z: asend.at[l, z], lambda o: ar.at[l, o], sem_a.at[0, l], sem_a.at[1, l])

    def a_wait(l):
        wait_bytes(ar.at[l, pl.ds(0, NR - 1)], sem_a.at[1, l])
        wait_bytes(ar.at[l, pl.ds(0, NR - 1)], sem_a.at[0, l])

    def r_send(l):
        rs[l, row] = rsend[l, row]
        for h in range(2):
            part_h = pl.ds(2 * h, 2)
            row_send(
                lambda z: rsend.at[l, z, part_h], lambda o: rs.at[l, o, part_h], sem_r.at[0, l, h], sem_r.at[1, l, h]
            )

    def r_wait(l, h):
        wait_bytes(rs.at[l, pl.ds(0, NR - 1), pl.ds(2 * h, 2)], sem_r.at[1, l, h])

    def r_wait_sent(l):
        for h in range(2):
            wait_bytes(rs.at[l, pl.ds(0, NR - 1), pl.ds(2 * h, 2)], sem_r.at[0, l, h])

    def col_send(src, dst, send_sem, recv_sem, pack):
        for i in range(cap):
            pack(src, dst, col * cap + i)
        dst[pl.ds(col * cap, cap)] = src[pl.ds(col * cap, cap)]

        def one(k):
            c = lax.rem(col + k, ncol)
            for i in range(cap):
                pack(src, dst, c * cap + i)
            pltpu.make_async_remote_copy(
                src_ref=src.at[pl.ds(c * cap, cap)], dst_ref=dst.at[pl.ds(col * cap, cap)],
                send_sem=send_sem, recv_sem=recv_sem,
                device_id={"col": c}, device_id_type=pl.DeviceIdType.MESH,
            ).start()

        steps = (ncol - 1) // 3

        @pl.loop(0, steps)
        def _(k):
            for i in range(3):
                one(3 * k + i + 1)
        for k in range(3 * steps + 1, ncol):
            one(k)

    def col_wait(dst, sem):
        wait_bytes(dst.at[pl.ds(0, SLOTS - cap)], sem)

    def fwd_pack_send(l, g):
        a, b = FWD_GROUPS[g]
        src, dst = fsend[g], frecv[g].at[l % 2]

        def pack(src, dst, s):
            k = tab[l, FSRC, s]
            if l == 0:
                src[s] = out[k, pl.ds(a, b - a)]
            else:
                src[s] = out[k, pl.ds(a, b - a)] + car[k, pl.ds(a, b - a)]
        col_send(src, dst, sem_fs.at[l, g], sem_fr.at[l, g], pack)

    def fwd_collect(l, g):
        a, b = FWD_GROUPS[g]
        dst = frecv[g].at[l % 2]
        col_wait(dst, sem_fr.at[l, g])
        col_wait(fsend[g], sem_fs.at[l, g])

        @pl.loop(0, SLOTS, unroll=4)
        def _(s):
            cum[s, pl.ds(0, b - a)] = dst[s] + cum[tab[l, PREV, s], pl.ds(0, b - a)]

        if g == 0:
            @pl.loop(0, SUP, unroll=4)
            def _(p):
                rsend[l + 1, p // OWN, p % OWN] = rhs[l + 1, p] - cum[tab[l, LAST, p], 0]
        else:
            @pl.loop(0, SUP, unroll=4)
            def _(p):
                car[p, pl.ds(a - 1, b - a)] = cum[tab[l, LAST, p], pl.ds(0, b - a)]

    def bwd_buffer(l, g):
        a, b = BWD_GROUPS[l][g]
        return bulk.at[:, pl.ds(0, b - a)] if b - a > 1 else bsend.at[l, g]

    def bwd_pack_send(l, g, source):
        src, dst = bwd_buffer(l, g), brecv[l][g]

        def pack(src, dst, s):
            src[s] = source(tab[l, BSRC, s])
        col_send(src, dst, sem_bs.at[l, g], sem_br.at[l, g], pack)

    def bwd_gather(l, g):
        a, b = BWD_GROUPS[l][g]
        dst = brecv[l][g]
        col_wait(dst, sem_br.at[l, g])
        col_wait(bwd_buffer(l, g), sem_bs.at[l, g])

        @pl.loop(0, SUP, unroll=4)
        def _(k):
            anct[l, k, pl.ds(a, b - a)] = dst[tab[l, POS, k]]

    def convert(l, low=0, high=SUP):
        place = (0, 0, 1, 1)[l]
        if low == 0:
            load_panels(l).wait()

        @pl.loop(low, high)
        def _(g):
            blocks = [stage[place, 0, g]]
            for d in range(1, ANC):
                blocks.append(stage[place, d, g] * pat[l, d - 1, g].astype(F32))
            whole = jnp.concatenate(blocks, axis=0)
            ph[l, g] = store_matrix(whole)
            pt[l, g] = store_matrix(whole.T)
        if l in (0, 3) and high == SUP:
            load_panels((1, None, None, 2)[l]).start()

    def ag_copy(l, c, t, way):
        origin = at_row(1 - t) if way == 0 else at_row(t - 1)
        return pltpu.make_async_remote_copy(
            src_ref=sol.at[l % 2, origin, c], dst_ref=sol.at[l % 2, origin, c],
            send_sem=sem_ag_s.at[l, c, t - 1, way], recv_sem=sem_ag_r.at[l, c, t - 1, way],
            device_id=rowdev(right if way == 0 else left), device_id_type=pl.DeviceIdType.MESH,
        )

    def ag_ways(c, t):
        return (0, 1) if t < 4 else (c % 2,)

    def product(l, g):
        out[g] = multiply(ph[l, g], sol[l % 2, g // OWN, g % OWN].reshape(8, 8, 128))

    def solve(l):
        for c in range(OWN):
            if c % 2 == 0:
                r_wait(l, c // 2)
            own[l, c] = multiply(dh[l, c], rs[l, :, c]).reshape(64, 128)
            sol[l % 2, row, c] = own[l, c]
            for way in ag_ways(c, 1):
                ag_copy(l, c, 1, way).start()
        r_wait_sent(l)

    def spread_step(l, t):
        if t == 0:
            for c in range(OWN):
                product(l, row * OWN + c)
            return
        for c in range(OWN):
            for way in ag_ways(c, t):
                ag_copy(l, c, t, way).wait_recv()
                if t < 4 and way in ag_ways(c, t + 1):
                    ag_copy(l, c, t + 1, way).start()
            for offset in (4,) if t == 4 else (-t, t):
                product(l, at_row(offset) * OWN + c)
        if t == 4:
            for t in range(1, 5):
                for c in range(OWN):
                    for way in ag_ways(c, t):
                        ag_copy(l, c, t, way).wait_send()

    def spread_solved(l, extra=None):
        for t in range(5):
            spread_step(l, t)
            if extra is not None and t < 4:
                extra(t)

    def rs_dest(t, way):
        return at_row(5 - t) if way == 0 else at_row(t - 5)

    def rs_ways(c, t):
        return (0, 1) if t > 1 else (c % 2,)

    def rs_copy(l, c, t, way):
        first = t == 1 or way not in rs_ways(c, t - 1)
        src = part.at[l % 2, rs_dest(t, way), c] if first else rsr.at[l % 2, way, t - 2, c]
        return pltpu.make_async_remote_copy(
            src_ref=src, dst_ref=rsr.at[l % 2, way, t - 1, c],
            send_sem=sem_rs_s.at[l, c, t - 1, way], recv_sem=sem_rs_r.at[l, c, t - 1, way],
            device_id=rowdev(right if way == 0 else left), device_id_type=pl.DeviceIdType.MESH,
        )

    def ring_step(l, t):
        for c in range(OWN):
            for way in rs_ways(c, t):
                if t > 1 and way in rs_ways(c, t - 1):
                    rs_copy(l, c, t - 1, way).wait_recv()
                    rsr[l % 2, way, t - 2, c] += part[l % 2, rs_dest(t, way), c]
                rs_copy(l, c, t, way).start()

    def ring_end(l):
        for c in range(OWN):
            for way in (0, 1):
                rs_copy(l, c, 4, way).wait_recv()
            tot[c] = part[l % 2, row, c] + rsr[l % 2, 0, 3, c] + rsr[l % 2, 1, 3, c]
        for c in range(OWN):
            for t in range(1, 5):
                for way in rs_ways(c, t):
                    rs_copy(l, c, t, way).wait_send()

    def partial_sums(l, low, high):
        @pl.loop(low, high, unroll=2)
        def _(g):
            part[l % 2, g // OWN, g % OWN] = multiply(pt[l, g], anc[g] if l == 3 else anct[l, g]).reshape(64, 128)

    def finish(l, c):
        reduced = (own[l, c] - tot[c]).reshape(8, 8, 128)
        if l < 3:
            reduced = reduced - multiply(p0[l, c], ar[l, :, c])
        xsend[l, :, c] = multiply(dt[l, c], reduced)
        if c % 2 == 1:
            h = c // 2
            part_h = pl.ds(2 * h, 2)
            solr[l, row, part_h] = xsend[l, row, part_h]
            row_send(
                lambda z: xsend.at[l, z, part_h], lambda o: solr.at[l, o, part_h], sem_x.at[0, l, h], sem_x.at[1, l, h]
            )

    def finish_wait(l):
        for h in range(2):
            for k in (1, 0):
                wait_bytes(solr.at[l, pl.ds(0, NR - 1), pl.ds(2 * h, 2)], sem_x.at[k, l, h])

    def emit(l):
        sol_out[l] = solr[l].reshape(SUP, 8, 128)

    def finish_all(l):
        for c in range(OWN):
            finish(l, c)

    def send_down(l):
        bwd_pack_send(l, 0, lambda k: solr[l + 1, k // OWN, pl.ds(k % OWN, 1)])

    def beside(l, t):
        if l == 0:
            if t < 2:
                convert(1, 16 * t, 16 * t + 16)
            else:
                partial_sums(3, 16 * t - 32, 16 * t - 16)
        elif l == 1:
            if t < 2:
                convert(2, 16 * t, 16 * t + 16)
            elif t == 2:
                ring_step(3, 2)
                bwd_gather(2, 1)
                bwd_pack_send(1, 2, lambda k: anct[2, k, pl.ds(1, 6)])
            else:
                fwd_collect(0, 1)
                fwd_collect(0, 2)
        else:
            if t < 2:
                partial_sums(2, 16 * t, 16 * t + 16)
            elif t == 2:
                bwd_gather(1, 2)
                bwd_pack_send(0, 3, lambda k: anct[1, k, pl.ds(2, 5)])
            else:
                fwd_collect(1, 1)
                fwd_collect(1, 2)

    rsend[0] = rhs[0].reshape(NR, OWN, 8, 128)
    r_send(0)
    dinv_send(0)
    cum[SLOTS] = jnp.zeros(cum.shape[1:], F32)
    bwd_pack_send(2, 1, lambda k: anc[k, pl.ds(0, 7)])

    @pl.loop(0, SUP)
    def _(g):
        car[g, 7] = jnp.zeros((8, 128), F32)
        for l in range(3):
            anct[l, g, 0] = jnp.zeros((8, 128), F32)
    convert(0)
    convert(3)
    dinv_wait(0)
    for l in range(LEVELS - 1):
        solve(l)
        spread_solved(l, functools.partial(beside, l))
        fwd_pack_send(l, 0)
        dinv_send(l + 1)
        ring_step(3, (1, 3, 4)[l])
        fwd_pack_send(l, 1)
        fwd_collect(l, 0)
        r_send(l + 1)
        p0_send(l)
        fwd_pack_send(l, 2)
        dinv_wait(l + 1)

    ring_step(2, 1)
    ring_end(3)
    solve(3)
    finish_all(3)
    ring_step(2, 2)
    ring_step(2, 3)
    p0_wait(2)
    finish_wait(3)
    send_down(2)
    spread_step(3, 0)
    ring_step(2, 4)
    p0_wait(1)
    emit(3)
    spread_step(3, 1)

    a_send(2)
    bwd_pack_send(1, 1, lambda k: asend[2, k // OWN, pl.ds(k % OWN, 1)])
    ring_end(2)
    spread_step(3, 2)
    a_wait(2)
    finish_all(2)
    p0_wait(0)
    bwd_gather(1, 1)
    partial_sums(1, 0, SUP)
    ring_step(1, 1)
    finish_wait(2)
    send_down(1)
    ring_step(1, 2)
    emit(2)
    ring_step(1, 3)

    a_send(1)
    bwd_pack_send(0, 1, lambda k: asend[1, k // OWN, pl.ds(k % OWN, 1)])
    bwd_pack_send(0, 2, lambda k: anct[1, k, pl.ds(1, 1)])
    ring_step(1, 4)
    bwd_gather(0, 3)
    ring_end(1)
    a_wait(1)
    finish_all(1)
    bwd_gather(0, 2)
    bwd_gather(0, 1)
    partial_sums(0, 0, SUP)
    ring_step(0, 1)
    finish_wait(1)
    send_down(0)
    ring_step(0, 2)
    emit(1)
    ring_step(0, 3)

    a_send(0)
    ring_step(0, 4)
    spread_step(3, 3)
    ring_end(0)
    a_wait(0)
    finish_all(0)
    spread_step(3, 4)
    fwd_collect(2, 1)
    fwd_collect(2, 2)

    @pl.loop(0, SUP)
    def _(g):
        bu_out[g, pl.ds(0, 7)] = out[g, pl.ds(0, 7)] + car[g, pl.ds(0, 7)]
        bu_out[g, 7] = out[g, 7]
    finish_wait(0)
    emit(0)


def tables(parent_owner, parent_local, ncol):
    cap = SLOTS // ncol
    owner = parent_owner[:, :, 0]
    here = jnp.arange(SUP, dtype=jnp.int32)
    same = (owner[:, :, None] == owner[:, None, :]) & (here[None, :, None] < here[None, None, :])
    pos = owner * cap + jnp.sum(same.astype(jnp.int32), axis=1)
    slots = jnp.arange(SLOTS, dtype=jnp.int32)
    hit = pos[:, None, :] == slots[None, :, None]
    fsrc = jnp.sum(jnp.where(hit, here[None, None, :], 0), axis=2)
    ids = jnp.sum(jnp.where(hit, parent_local[:, None, :] + 1, 0), axis=2)
    ids = lax.all_to_all(ids.reshape(3, ncol, cap), "col", split_axis=1, concat_axis=1, tiled=True).reshape(3, SLOTS)
    equal = (ids[:, :, None] == ids[:, None, :]) & (slots[None, None, :] < slots[None, :, None])
    prev = jnp.max(jnp.where(equal, slots[None, None, :], -1), axis=2)
    prev = jnp.where(prev < 0, SLOTS, prev)
    mine = ids[:, None, :] == here[None, :, None] + 1
    last = jnp.max(jnp.where(mine, slots[None, None, :], -1), axis=2)
    last = jnp.where(last < 0, SLOTS, last)
    bsrc = jnp.maximum(ids - 1, 0)
    wide = lambda x: jnp.pad(x, ((0, 0), (0, SLOTS - x.shape[1])))
    return jnp.stack([fsrc, wide(pos), prev, wide(last), bsrc], axis=1)


def per_device(ncol, rhs, dinv, panels, pattern, parent_owner, parent_local, ancestor_solution):
    tab = tables(parent_owner, parent_local, ncol)
    rhs_p = rhs.reshape(LEVELS, 2, 8, SUP, 64).transpose(0, 3, 2, 1, 4).reshape(LEVELS, SUP, 8, 128)
    anc_p = ancestor_solution.reshape(2, 8, SUP, ANC, 64).transpose(2, 3, 1, 0, 4).reshape(SUP, ANC, 8, 128)
    vmem = pl.BlockSpec(memory_space=pltpu.VMEM)
    smem = pl.BlockSpec(memory_space=pltpu.SMEM)
    anywhere = pl.BlockSpec(memory_space=pl.ANY)
    sems = pltpu.SemaphoreType.DMA
    tile = (8, 128)
    fsend = tuple(pltpu.VMEM((SLOTS, b - a) + tile, F32) for a, b in FWD_GROUPS)
    frecv = tuple(pltpu.VMEM((2, SLOTS, b - a) + tile, F32) for a, b in FWD_GROUPS)
    bbuf = tuple(tuple(pltpu.VMEM((SLOTS, b - a) + tile, F32) for a, b in groups) for groups in BWD_GROUPS)
    sol, bu = pl.pallas_call(
        functools.partial(kernel, ncol),
        out_shape=(
            jax.ShapeDtypeStruct((LEVELS, SUP) + tile, F32),
            jax.ShapeDtypeStruct((SUP, ANC) + tile, F32),
        ),
        in_specs=[smem, smem, vmem, vmem, anywhere, anywhere],
        out_specs=(vmem, vmem),
        scratch_shapes=[
            pltpu.VMEM((2, ANC, SUP, 16, 128), F32),
            pltpu.VMEM((LEVELS, SUP, 128, 256), BF16),
            pltpu.VMEM((LEVELS, SUP, 128, 256), BF16),
            pltpu.VMEM((LEVELS, NR, OWN, 16, 128), F32),
            pltpu.VMEM((LEVELS, OWN, 128, 256), BF16),
            pltpu.VMEM((LEVELS, OWN, 128, 256), BF16),
            pltpu.VMEM((3, NR, OWN, 16, 128), F32),
            pltpu.VMEM((3, OWN, 128, 256), BF16),
            pltpu.VMEM((LEVELS, NR, OWN) + tile, F32),
            pltpu.VMEM((LEVELS, NR, OWN) + tile, F32),
            pltpu.VMEM((3, NR, OWN) + tile, F32),
            pltpu.VMEM((3, NR, OWN) + tile, F32),
            pltpu.VMEM((LEVELS, OWN, 64, 128), F32),
            pltpu.VMEM((2, NR, OWN, 64, 128), F32),
            pltpu.VMEM((SUP, ANC) + tile, F32),
            pltpu.VMEM((SUP, ANC) + tile, F32),
            pltpu.VMEM((SLOTS + 1, 6) + tile, F32),
            fsend, frecv, pltpu.VMEM((3, 3, SLOTS, 1) + tile, F32), pltpu.VMEM((SLOTS, 7) + tile, F32), bbuf,
            pltpu.VMEM((3, SUP, ANC) + tile, F32),
            pltpu.VMEM((2, NR, OWN, 64, 128), F32),
            pltpu.VMEM((2, 2, 4, OWN, 64, 128), F32),
            pltpu.VMEM((OWN, 64, 128), F32),
            pltpu.VMEM((LEVELS, NR, OWN) + tile, F32),
            pltpu.VMEM((LEVELS, NR, OWN) + tile, F32),
            sems((2,)), sems((3, LEVELS)), sems((3, 3)), sems((2, 3)), sems((2, LEVELS, 2)),
            sems((LEVELS, OWN, 4, 2)), sems((LEVELS, OWN, 4, 2)),
            sems((3, 3)), sems((3, 3)), sems((3, 4)), sems((3, 4)),
            sems((LEVELS, OWN, 4, 2)), sems((LEVELS, OWN, 4, 2)), sems((2, LEVELS, 2)),
        ],
        compiler_params=pltpu.CompilerParams(
            collective_id=0, has_side_effects=True, vmem_limit_bytes=60 * 1024 * 1024
        ),
        cost_estimate=pl.CostEstimate(flops=4 * 10**9, bytes_accessed=12 * 10**6, transcendentals=0),
    )(tab, pattern, rhs_p, anc_p, dinv, panels)
    solution = sol.reshape(LEVELS, SUP, 8, 2, 64).transpose(0, 3, 2, 1, 4).reshape(LEVELS, 16, SUP, 64)
    boundary = bu.reshape(SUP, ANC, 8, 2, 64).transpose(3, 2, 0, 1, 4).reshape(16, SUP, ANC, 64)
    return solution, boundary


def solution(mesh):
    placed = (
        P(None, "row", "col", None),
        P(None, "col", "row", None),
        P(None, None, "col", "row", None),
        P(None, None, "col"),
        P(None, "col", None),
        P(None, "col"),
        P("row", "col", None, None),
    )
    return jax.shard_map(
        functools.partial(per_device, mesh.shape["col"]),
        mesh=mesh,
        in_specs=placed,
        out_specs=(P(None, "row", "col", None), P("row", "col", None, None)),
        check_vma=False,
    )
```

```python
import functools

import jax
import jax.numpy as jnp
from jax import lax
from jax.experimental import pallas as pl
from jax.experimental.pallas import tpu as pltpu
from jax.sharding import PartitionSpec as P

F32 = jnp.float32
BF16 = jnp.bfloat16
LEVELS = 4
ANC = 8
SUP = 32
SLOTS = 64
NR = 8
OWN = SUP // NR
FWD_GROUPS = ((0, 1), (1, 2), (2, 3), (3, 4), (4, 6), (6, 8))
BWD_GROUPS = (
    ((0, 1), (1, 2), (2, 3), (3, 5), (5, 7), (7, 8)),
    ((0, 1), (1, 2), (2, 4), (4, 6), (6, 8)),
    ((0, 1), (1, 8)),
)
FSRC, POS, PREV, LAST, BSRC = range(5)


def low_lanes(shape):
    return lax.broadcasted_iota(jnp.int32, shape, len(shape) - 1) < 64


def swap_halves(x):
    return pltpu.roll(x.reshape(-1, 128), 64, 1).reshape(x.shape)


def split(x):
    high = x.astype(BF16).astype(F32)
    return high, x - high


def store_matrix(block):
    high, low = split(block)
    return jnp.concatenate([high.astype(BF16), low.astype(BF16)], axis=1)


def multiply(matrix, tiles):
    low = low_lanes((8, 128))
    high, rest = split(tiles)
    high_r, rest_r = swap_halves(high), swap_halves(rest)
    rows = []
    for z in range(8):
        rows += [jnp.where(low, high[z], rest_r[z]), jnp.where(low, high_r[z], rest[z])]
    weights = jnp.concatenate(rows, axis=0).astype(BF16)
    weights = jnp.concatenate([weights, weights], axis=0)
    o = jnp.dot(matrix, weights, preferred_element_type=F32).reshape(8, 2, 8, 128)
    low = low_lanes((8, 8, 128))
    return jnp.where(low, o[:, 0], o[:, 1]) + swap_halves(jnp.where(low, o[:, 1], o[:, 0]))


def kernel(
    ncol, tab, pat, rhs, anc, dinv, panels, sol_out, bu_out,
    stage, ph, pt, dv, dh, dt, pv, p0, rsend, rs, asend, ar, own, sol, out, car, cum, fsend, frecv, bsend, bulk, brecv, anct,
    part, rsr, tot, xsend, solr,
    sem_stage, sem_dv, sem_p, sem_a, sem_r, sem_ag_s, sem_ag_r, sem_fs, sem_fr, sem_bs, sem_br, sem_rs_s, sem_rs_r, sem_x,
):
    row, col = lax.axis_index("row"), lax.axis_index("col")
    cap = SLOTS // ncol
    right, left = lax.rem(row + 1, NR), lax.rem(row + NR - 1, NR)

    def rowdev(z):
        return {"row": z}

    def at_row(offset):
        return lax.rem(row + offset + 2 * NR, NR)

    barrier = pltpu.get_barrier_semaphore()

    @pl.loop(1, NR)
    def _(k):
        pl.semaphore_signal(barrier, inc=1, device_id=rowdev(lax.rem(row + k, NR)), device_id_type=pl.DeviceIdType.MESH)

    @pl.loop(1, ncol)
    def _(k):
        pl.semaphore_signal(barrier, inc=1, device_id={"col": lax.rem(col + k, ncol)}, device_id_type=pl.DeviceIdType.MESH)

    def load_panels(l):
        place = (0, 0, 1, 1)[l]
        return pltpu.make_async_copy(panels.at[l], stage.at[place], sem_stage.at[place])

    load_panels(0).start()
    load_panels(3).start()
    pl.semaphore_wait(barrier, NR - 1 + ncol - 1)

    def out_at(l, g, a, b):
        if l < 2:
            return out.at[l, g, pl.ds(a, b - a)]
        return stage.at[0, pl.ds(a, b - a), g, pl.ds(8 * (l - 2), 8)]

    def car_at(l, g, a, b):
        if l == 1:
            return car.at[g, pl.ds(a, b - a)]
        return stage.at[1, pl.ds(a, b - a), g, pl.ds(8 * (l - 2), 8)]

    def row_send(src, dst, send_sem, recv_sem):
        for k in (4, 3, 5, 2, 6, 1, 7):
            z = lax.rem(row + k, NR)
            pltpu.make_async_remote_copy(
                src_ref=src(z), dst_ref=dst(row), send_sem=send_sem, recv_sem=recv_sem,
                device_id=rowdev(z), device_id_type=pl.DeviceIdType.MESH,
            ).start()

    def wait_bytes(ref, sem):
        pltpu.make_async_copy(ref, ref, sem).wait()

    def dinv_send(l):
        row_send(lambda z: dinv.at[l, pl.ds(z * OWN, OWN)], lambda o: dv.at[l, o], sem_dv.at[0, l], sem_dv.at[1, l])
        pltpu.make_async_copy(dinv.at[l, pl.ds(row * OWN, OWN)], dv.at[l, row], sem_dv.at[2, l]).start()

    def dinv_wait(l):
        wait_bytes(dv.at[l, pl.ds(0, NR - 1)], sem_dv.at[0, l])
        wait_bytes(dv.at[l, pl.ds(0, NR - 1)], sem_dv.at[1, l])
        wait_bytes(dv.at[l, 0], sem_dv.at[2, l])
        for j in range(OWN):
            whole = dv[l, :, j].reshape(128, 128)
            dh[l, j] = store_matrix(whole)
            dt[l, j] = store_matrix(whole.T)

    def p0_send(l):
        row_send(lambda z: panels.at[l, 0, pl.ds(z * OWN, OWN)], lambda o: pv.at[l, o], sem_p.at[0, l], sem_p.at[1, l])
        pltpu.make_async_copy(panels.at[l, 0, pl.ds(row * OWN, OWN)], pv.at[l, row], sem_p.at[2, l]).start()

    def p0_wait(l):
        wait_bytes(pv.at[l, pl.ds(0, NR - 1)], sem_p.at[0, l])
        wait_bytes(pv.at[l, pl.ds(0, NR - 1)], sem_p.at[1, l])
        wait_bytes(pv.at[l, 0], sem_p.at[2, l])
        for j in range(OWN):
            p0[l, j] = store_matrix(pv[l, :, j].reshape(128, 128).T)

    def a_send(l):
        col_wait(brecv[l][0], sem_br.at[l, 0])
        col_wait(bwd_buffer(l, 0), sem_bs.at[l, 0])

        @pl.loop(0, SUP, unroll=4)
        def _(k):
            asend[l, k // OWN, k % OWN] = brecv[l][0][tab[l, POS, k], 0]
        ar[l, row] = asend[l, row]
        row_send(lambda z: asend.at[l, z], lambda o: ar.at[l, o], sem_a.at[0, l], sem_a.at[1, l])

    def a_wait(l):
        wait_bytes(ar.at[l, pl.ds(0, NR - 1)], sem_a.at[1, l])
        wait_bytes(ar.at[l, pl.ds(0, NR - 1)], sem_a.at[0, l])

    def r_send(l):
        rs[l, row] = rsend[l, row]
        for h in range(2):
            part_h = pl.ds(2 * h, 2)
            row_send(
                lambda z: rsend.at[l, z, part_h], lambda o: rs.at[l, o, part_h], sem_r.at[0, l, h], sem_r.at[1, l, h]
            )

    def r_wait(l, h):
        wait_bytes(rs.at[l, pl.ds(0, NR - 1), pl.ds(2 * h, 2)], sem_r.at[1, l, h])

    def r_wait_sent(l):
        for h in range(2):
            wait_bytes(rs.at[l, pl.ds(0, NR - 1), pl.ds(2 * h, 2)], sem_r.at[0, l, h])

    def col_send(src, dst, send_sem, recv_sem, pack):
        for i in range(cap):
            pack(src, dst, col * cap + i)
        dst[pl.ds(col * cap, cap)] = src[pl.ds(col * cap, cap)]

        def one(c):
            for i in range(cap):
                pack(src, dst, c * cap + i)
            pltpu.make_async_remote_copy(
                src_ref=src.at[pl.ds(c * cap, cap)], dst_ref=dst.at[pl.ds(col * cap, cap)],
                send_sem=send_sem, recv_sem=recv_sem,
                device_id={"col": c}, device_id_type=pl.DeviceIdType.MESH,
            ).start()

        if ncol == 32:
            x, y, core = col // 8, lax.rem(col // 2, 4), lax.rem(col, 2)

            @pl.loop(1, 16, unroll=3)
            def _(k):
                chip = lax.rem(x + k, 4) * 8 + lax.rem(y + k + k // 4, 4) * 2
                one(chip + core)
                one(chip + 1 - core)
            one(col + 1 - 2 * core)
        else:
            @pl.loop(1, ncol)
            def _(k):
                one(lax.rem(col + k, ncol))

    def col_wait(dst, sem):
        wait_bytes(dst.at[pl.ds(0, SLOTS - cap)], sem)

    def fwd_pack_send(l, g):
        a, b = FWD_GROUPS[g]
        src, dst = fsend[g], frecv[g].at[l % 2]

        def pack(src, dst, s):
            k = tab[l, FSRC, s]
            if l == 0:
                src[s] = out_at(l, k, a, b)[...]
            else:
                src[s] = out_at(l, k, a, b)[...] + car_at(l, k, a, b)[...]
        col_send(src, dst, sem_fs.at[l, g], sem_fr.at[l, g], pack)

    def fwd_collect(l, g):
        a, b = FWD_GROUPS[g]
        dst = frecv[g].at[l % 2]
        col_wait(dst, sem_fr.at[l, g])
        col_wait(fsend[g], sem_fs.at[l, g])

        @pl.loop(0, SLOTS, unroll=4)
        def _(s):
            cum[s, pl.ds(0, b - a)] = dst[s] + cum[tab[l, PREV, s], pl.ds(0, b - a)]

        if g == 0:
            @pl.loop(0, SUP, unroll=4)
            def _(p):
                rsend[l + 1, p // OWN, p % OWN] = rhs[l + 1, p] - cum[tab[l, LAST, p], 0]
        else:
            @pl.loop(0, SUP, unroll=4)
            def _(p):
                car_at(l + 1, p, a - 1, b - 1)[...] = cum[tab[l, LAST, p], pl.ds(0, b - a)]

    def bwd_buffer(l, g):
        a, b = BWD_GROUPS[l][g]
        if b - a == 1 and g < 3:
            return bsend.at[l, g]
        return bulk.at[:, pl.ds(a - (3, 2, 1)[l], b - a)]

    def bwd_pack_send(l, g, source):
        src, dst = bwd_buffer(l, g), brecv[l][g]

        def pack(src, dst, s):
            src[s] = source(tab[l, BSRC, s])
        col_send(src, dst, sem_bs.at[l, g], sem_br.at[l, g], pack)

    def bwd_gather(l, g):
        a, b = BWD_GROUPS[l][g]
        dst = brecv[l][g]
        col_wait(dst, sem_br.at[l, g])
        col_wait(bwd_buffer(l, g), sem_bs.at[l, g])

        @pl.loop(0, SUP, unroll=4)
        def _(k):
            anct[l, k, pl.ds(a, b - a)] = dst[tab[l, POS, k]]

    def convert(l, low=0, high=SUP):
        place = (0, 0, 1, 1)[l]
        if low == 0:
            load_panels(l).wait()

        @pl.loop(low, high)
        def _(g):
            blocks = [stage[place, 0, g]]
            for d in range(1, ANC):
                blocks.append(stage[place, d, g] * pat[l, d - 1, g].astype(F32))
            whole = jnp.concatenate(blocks, axis=0)
            ph[l, g] = store_matrix(whole)
            pt[l, g] = store_matrix(whole.T)
        if l in (0, 3) and high == SUP:
            load_panels((1, None, None, 2)[l]).start()

    def ag_copy(l, c, t, way):
        origin = at_row(1 - t) if way == 0 else at_row(t - 1)
        return pltpu.make_async_remote_copy(
            src_ref=sol.at[l % 2, origin, c], dst_ref=sol.at[l % 2, origin, c],
            send_sem=sem_ag_s.at[l, c, t - 1, way], recv_sem=sem_ag_r.at[l, c, t - 1, way],
            device_id=rowdev(right if way == 0 else left), device_id_type=pl.DeviceIdType.MESH,
        )

    def ag_ways(c, t):
        return (0, 1) if t < 4 else (c % 2,)

    def product(l, g):
        out_at(l, g, 0, 8)[...] = multiply(ph[l, g], sol[l % 2, g // OWN, g % OWN].reshape(8, 8, 128))

    def solve(l):
        for c in range(OWN):
            if c % 2 == 0:
                r_wait(l, c // 2)
            own[l, c] = multiply(dh[l, c], rs[l, :, c]).reshape(64, 128)
            sol[l % 2, row, c] = own[l, c]
            for way in ag_ways(c, 1):
                ag_copy(l, c, 1, way).start()
        r_wait_sent(l)

    def spread_step(l, t):
        if t == 0:
            for c in range(OWN):
                product(l, row * OWN + c)
            return
        for c in range(OWN):
            for way in ag_ways(c, t):
                ag_copy(l, c, t, way).wait_recv()
                if t < 4 and way in ag_ways(c, t + 1):
                    ag_copy(l, c, t + 1, way).start()
            for offset in (4,) if t == 4 else (-t, t):
                product(l, at_row(offset) * OWN + c)
        if t == 4:
            for t in range(1, 5):
                for c in range(OWN):
                    for way in ag_ways(c, t):
                        ag_copy(l, c, t, way).wait_send()

    def spread_solved(l, extra=None):
        for t in range(5):
            spread_step(l, t)
            if extra is not None and t < 4:
                extra(t)

    def rs_dest(t, way):
        return at_row(5 - t) if way == 0 else at_row(t - 5)

    def rs_ways(c, t):
        return (0, 1) if t > 1 else (c % 2,)

    def rs_copy(l, c, t, way):
        first = t == 1 or way not in rs_ways(c, t - 1)
        src = part.at[l % 2, rs_dest(t, way), c] if first else rsr.at[l % 2, way, t - 2, c]
        return pltpu.make_async_remote_copy(
            src_ref=src, dst_ref=rsr.at[l % 2, way, t - 1, c],
            send_sem=sem_rs_s.at[l, c, t - 1, way], recv_sem=sem_rs_r.at[l, c, t - 1, way],
            device_id=rowdev(right if way == 0 else left), device_id_type=pl.DeviceIdType.MESH,
        )

    def ring_step(l, t):
        for c in range(OWN):
            for way in rs_ways(c, t):
                if t > 1 and way in rs_ways(c, t - 1):
                    rs_copy(l, c, t - 1, way).wait_recv()
                    rsr[l % 2, way, t - 2, c] += part[l % 2, rs_dest(t, way), c]
                rs_copy(l, c, t, way).start()

    def ring_end(l):
        for c in range(OWN):
            for way in (0, 1):
                rs_copy(l, c, 4, way).wait_recv()
            tot[c] = part[l % 2, row, c] + rsr[l % 2, 0, 3, c] + rsr[l % 2, 1, 3, c]
        for c in range(OWN):
            for t in range(1, 5):
                for way in rs_ways(c, t):
                    rs_copy(l, c, t, way).wait_send()

    def partial_sums(l, low, high):
        @pl.loop(low, high, unroll=2)
        def _(g):
            part[l % 2, g // OWN, g % OWN] = multiply(pt[l, g], anc[g] if l == 3 else anct[l, g]).reshape(64, 128)

    def finish(l, c):
        reduced = (own[l, c] - tot[c]).reshape(8, 8, 128)
        if l < 3:
            reduced = reduced - multiply(p0[l, c], ar[l, :, c])
        xsend[l, :, c] = multiply(dt[l, c], reduced)
        if c % 2 == 1:
            h = c // 2
            part_h = pl.ds(2 * h, 2)
            solr[l, row, part_h] = xsend[l, row, part_h]
            row_send(
                lambda z: xsend.at[l, z, part_h], lambda o: solr.at[l, o, part_h], sem_x.at[0, l, h], sem_x.at[1, l, h]
            )

    def finish_wait(l):
        for h in range(2):
            for k in (1, 0):
                wait_bytes(solr.at[l, pl.ds(0, NR - 1), pl.ds(2 * h, 2)], sem_x.at[k, l, h])

    def emit(l):
        sol_out[l] = solr[l].reshape(SUP, 8, 128)

    def finish_all(l):
        for c in range(OWN):
            finish(l, c)

    def send_down(l):
        bwd_pack_send(l, 0, lambda k: solr[l + 1, k // OWN, pl.ds(k % OWN, 1)])

    def beside(l, t):
        if l == 0:
            if t < 2:
                convert(1, 16 * t, 16 * t + 16)
            else:
                partial_sums(3, 16 * t - 32, 16 * t - 16)
        elif l == 1:
            if t < 2:
                convert(2, 16 * t, 16 * t + 16)
            elif t == 2:
                ring_step(3, 2)
                fwd_collect(0, 1)
            else:
                fwd_collect(0, 2)

                @pl.loop(0, SUP)
                def _(g):
                    car_at(2, g, 7, 8)[...] = jnp.zeros((1, 8, 128), F32)
        else:
            if t < 2:
                partial_sums(2, 16 * t, 16 * t + 16)
            elif t == 2:
                fwd_collect(1, 1)
            else:
                fwd_collect(1, 2)

    def relay(l, g):
        a, b = BWD_GROUPS[l][g]
        bwd_pack_send(l, g, lambda k: anct[l + 1, k, pl.ds(a - 1, b - a)])

    rsend[0] = rhs[0].reshape(NR, OWN, 8, 128)
    r_send(0)
    dinv_send(0)
    cum[SLOTS] = jnp.zeros(cum.shape[1:], F32)
    bwd_pack_send(2, 1, lambda k: anc[k, pl.ds(0, 7)])

    @pl.loop(0, SUP)
    def _(g):
        car[g, 7] = jnp.zeros((8, 128), F32)
        for l in range(3):
            anct[l, g, 0] = jnp.zeros((8, 128), F32)
    convert(0)
    convert(3)
    dinv_wait(0)
    for l in range(LEVELS - 1):
        solve(l)
        spread_solved(l, functools.partial(beside, l))
        fwd_pack_send(l, 0)
        dinv_send(l + 1)
        ring_step(3, (1, 3, 4)[l])
        fwd_pack_send(l, 1)
        fwd_collect(l, 0)
        r_send(l + 1)
        p0_send(l)
        if l == 0:
            fwd_pack_send(0, 2)
            fwd_pack_send(0, 3)
            bwd_gather(2, 1)
            relay(1, 2)
            fwd_pack_send(0, 4)
        if l == 1:
            fwd_collect(0, 3)
            fwd_pack_send(1, 2)
            fwd_collect(0, 4)
            fwd_pack_send(1, 3)
            relay(1, 3)
            relay(1, 4)
        if l == 2:
            bwd_gather(1, 2)
            relay(0, 3)
        dinv_wait(l + 1)

    ring_step(2, 1)
    ring_end(3)
    solve(3)
    finish_all(3)
    bwd_gather(1, 3)
    relay(0, 4)
    ring_step(2, 2)
    ring_step(2, 3)
    p0_wait(2)
    finish_wait(3)
    send_down(2)
    fwd_pack_send(0, 5)
    spread_step(3, 0)
    ring_step(2, 4)
    p0_wait(1)
    emit(3)
    spread_step(3, 1)

    a_send(2)
    bwd_pack_send(1, 1, lambda k: asend[2, k // OWN, pl.ds(k % OWN, 1)])
    bwd_gather(1, 4)
    relay(0, 5)
    ring_end(2)
    spread_step(3, 2)
    a_wait(2)
    finish_all(2)
    p0_wait(0)
    fwd_collect(0, 5)
    fwd_pack_send(1, 4)
    bwd_gather(1, 1)
    partial_sums(1, 0, SUP)
    ring_step(1, 1)
    finish_wait(2)
    send_down(1)
    fwd_pack_send(1, 5)
    ring_step(1, 2)
    emit(2)
    ring_step(1, 3)

    a_send(1)
    bwd_pack_send(0, 1, lambda k: asend[1, k // OWN, pl.ds(k % OWN, 1)])
    relay(0, 2)
    fwd_collect(1, 3)
    fwd_pack_send(2, 2)
    ring_step(1, 4)
    bwd_gather(0, 3)
    bwd_gather(0, 4)
    ring_end(1)
    a_wait(1)
    finish_all(1)
    bwd_gather(0, 5)
    bwd_gather(0, 1)
    bwd_gather(0, 2)
    partial_sums(0, 0, SUP)
    ring_step(0, 1)
    finish_wait(1)
    send_down(0)
    fwd_collect(1, 4)
    fwd_pack_send(2, 3)
    ring_step(0, 2)
    fwd_collect(1, 5)
    fwd_pack_send(2, 4)
    fwd_pack_send(2, 5)
    emit(1)
    ring_step(0, 3)

    a_send(0)
    ring_step(0, 4)
    spread_step(3, 3)
    ring_end(0)
    a_wait(0)
    finish_all(0)
    spread_step(3, 4)
    for g in range(1, 6):
        fwd_collect(2, g)

    @pl.loop(0, SUP)
    def _(g):
        bu_out[g, pl.ds(0, 7)] = out_at(3, g, 0, 7)[...] + car_at(3, g, 0, 7)[...]
        bu_out[g, pl.ds(7, 1)] = out_at(3, g, 7, 8)[...]
    finish_wait(0)
    emit(0)


def tables(parent_owner, parent_local, ncol):
    cap = SLOTS // ncol
    owner = parent_owner[:, :, 0]
    here = jnp.arange(SUP, dtype=jnp.int32)
    same = (owner[:, :, None] == owner[:, None, :]) & (here[None, :, None] < here[None, None, :])
    pos = owner * cap + jnp.sum(same.astype(jnp.int32), axis=1)
    slots = jnp.arange(SLOTS, dtype=jnp.int32)
    hit = pos[:, None, :] == slots[None, :, None]
    fsrc = jnp.sum(jnp.where(hit, here[None, None, :], 0), axis=2)
    ids = jnp.sum(jnp.where(hit, parent_local[:, None, :] + 1, 0), axis=2)
    ids = lax.all_to_all(ids.reshape(3, ncol, cap), "col", split_axis=1, concat_axis=1, tiled=True).reshape(3, SLOTS)
    equal = (ids[:, :, None] == ids[:, None, :]) & (slots[None, None, :] < slots[None, :, None])
    prev = jnp.max(jnp.where(equal, slots[None, None, :], -1), axis=2)
    prev = jnp.where(prev < 0, SLOTS, prev)
    mine = ids[:, None, :] == here[None, :, None] + 1
    last = jnp.max(jnp.where(mine, slots[None, None, :], -1), axis=2)
    last = jnp.where(last < 0, SLOTS, last)
    bsrc = jnp.maximum(ids - 1, 0)
    wide = lambda x: jnp.pad(x, ((0, 0), (0, SLOTS - x.shape[1])))
    return jnp.stack([fsrc, wide(pos), prev, wide(last), bsrc], axis=1)


def per_device(ncol, rhs, dinv, panels, pattern, parent_owner, parent_local, ancestor_solution):
    tab = tables(parent_owner, parent_local, ncol)
    rhs_p = rhs.reshape(LEVELS, 2, 8, SUP, 64).transpose(0, 3, 2, 1, 4).reshape(LEVELS, SUP, 8, 128)
    anc_p = ancestor_solution.reshape(2, 8, SUP, ANC, 64).transpose(2, 3, 1, 0, 4).reshape(SUP, ANC, 8, 128)
    vmem = pl.BlockSpec(memory_space=pltpu.VMEM)
    smem = pl.BlockSpec(memory_space=pltpu.SMEM)
    anywhere = pl.BlockSpec(memory_space=pl.ANY)
    sems = pltpu.SemaphoreType.DMA
    tile = (8, 128)
    fsend = tuple(pltpu.VMEM((SLOTS, b - a) + tile, F32) for a, b in FWD_GROUPS)
    frecv = tuple(pltpu.VMEM((2, SLOTS, b - a) + tile, F32) for a, b in FWD_GROUPS)
    bbuf = tuple(tuple(pltpu.VMEM((SLOTS, b - a) + tile, F32) for a, b in groups) for groups in BWD_GROUPS)
    sol, bu = pl.pallas_call(
        functools.partial(kernel, ncol),
        out_shape=(
            jax.ShapeDtypeStruct((LEVELS, SUP) + tile, F32),
            jax.ShapeDtypeStruct((SUP, ANC) + tile, F32),
        ),
        in_specs=[smem, smem, vmem, vmem, anywhere, anywhere],
        out_specs=(vmem, vmem),
        scratch_shapes=[
            pltpu.VMEM((2, ANC, SUP, 16, 128), F32),
            pltpu.VMEM((LEVELS, SUP, 128, 256), BF16),
            pltpu.VMEM((LEVELS, SUP, 128, 256), BF16),
            pltpu.VMEM((LEVELS, NR, OWN, 16, 128), F32),
            pltpu.VMEM((LEVELS, OWN, 128, 256), BF16),
            pltpu.VMEM((LEVELS, OWN, 128, 256), BF16),
            pltpu.VMEM((3, NR, OWN, 16, 128), F32),
            pltpu.VMEM((3, OWN, 128, 256), BF16),
            pltpu.VMEM((LEVELS, NR, OWN) + tile, F32),
            pltpu.VMEM((LEVELS, NR, OWN) + tile, F32),
            pltpu.VMEM((3, NR, OWN) + tile, F32),
            pltpu.VMEM((3, NR, OWN) + tile, F32),
            pltpu.VMEM((LEVELS, OWN, 64, 128), F32),
            pltpu.VMEM((2, NR, OWN, 64, 128), F32),
            pltpu.VMEM((2, SUP, ANC) + tile, F32),
            pltpu.VMEM((SUP, ANC) + tile, F32),
            pltpu.VMEM((SLOTS + 1, 2) + tile, F32),
            fsend, frecv, pltpu.VMEM((3, 3, SLOTS, 1) + tile, F32), pltpu.VMEM((SLOTS, 7) + tile, F32), bbuf,
            pltpu.VMEM((3, SUP, ANC) + tile, F32),
            pltpu.VMEM((2, NR, OWN, 64, 128), F32),
            pltpu.VMEM((2, 2, 4, OWN, 64, 128), F32),
            pltpu.VMEM((OWN, 64, 128), F32),
            pltpu.VMEM((LEVELS, NR, OWN) + tile, F32),
            pltpu.VMEM((LEVELS, NR, OWN) + tile, F32),
            sems((2,)), sems((3, LEVELS)), sems((3, 3)), sems((2, 3)), sems((2, LEVELS, 2)),
            sems((LEVELS, OWN, 4, 2)), sems((LEVELS, OWN, 4, 2)),
            sems((3, 6)), sems((3, 6)), sems((3, 6)), sems((3, 6)),
            sems((LEVELS, OWN, 4, 2)), sems((LEVELS, OWN, 4, 2)), sems((2, LEVELS, 2)),
        ],
        compiler_params=pltpu.CompilerParams(
            collective_id=0, has_side_effects=True, vmem_limit_bytes=60 * 1024 * 1024
        ),
        cost_estimate=pl.CostEstimate(flops=4 * 10**9, bytes_accessed=12 * 10**6, transcendentals=0),
    )(tab, pattern, rhs_p, anc_p, dinv, panels)
    solution = sol.reshape(LEVELS, SUP, 8, 2, 64).transpose(0, 3, 2, 1, 4).reshape(LEVELS, 16, SUP, 64)
    boundary = bu.reshape(SUP, ANC, 8, 2, 64).transpose(3, 2, 0, 1, 4).reshape(16, SUP, ANC, 64)
    return solution, boundary


def solution(mesh):
    placed = (
        P(None, "row", "col", None),
        P(None, "col", "row", None),
        P(None, None, "col", "row", None),
        P(None, None, "col"),
        P(None, "col", None),
        P(None, "col"),
        P("row", "col", None, None),
    )
    return jax.shard_map(
        functools.partial(per_device, mesh.shape["col"]),
        mesh=mesh,
        in_specs=placed,
        out_specs=(P(None, "row", "col", None), P("row", "col", None, None)),
        check_vma=False,
    )
```

```python
import functools

import jax
import jax.numpy as jnp
from jax import lax
from jax.experimental import pallas as pl
from jax.experimental.pallas import tpu as pltpu
from jax.sharding import PartitionSpec as P

F32 = jnp.float32
BF16 = jnp.bfloat16
LEVELS = 4
ANC = 8
SUP = 32
SLOTS = 64
NR = 8
OWN = SUP // NR
FWD_GROUPS = ((0, 1), (1, 2), (2, 3), (3, 4), (4, 6), (6, 8))
BWD_GROUPS = (
    ((0, 1), (1, 2), (2, 3), (3, 5), (5, 7), (7, 8)),
    ((0, 1), (1, 2), (2, 4), (4, 6), (6, 8)),
    ((0, 1), (1, 8)),
)
FSRC, POS = range(2)
PREV, LAST, BSRC = range(3)


def low_lanes(shape):
    return lax.broadcasted_iota(jnp.int32, shape, len(shape) - 1) < 64


def swap_halves(x):
    return pltpu.roll(x.reshape(-1, 128), 64, 1).reshape(x.shape)


def split(x):
    high = x.astype(BF16).astype(F32)
    return high, x - high


def store_matrix(block):
    high, low = split(block)
    return jnp.concatenate([high.astype(BF16), low.astype(BF16)], axis=1)


def multiply(matrix, tiles):
    low = low_lanes((8, 128))
    high, rest = split(tiles)
    high_r, rest_r = swap_halves(high), swap_halves(rest)
    rows = []
    for z in range(8):
        rows += [jnp.where(low, high[z], rest_r[z]), jnp.where(low, high_r[z], rest[z])]
    weights = jnp.concatenate(rows, axis=0).astype(BF16)
    weights = jnp.concatenate([weights, weights], axis=0)
    o = jnp.dot(matrix, weights, preferred_element_type=F32).reshape(8, 2, 8, 128)
    low = low_lanes((8, 8, 128))
    return jnp.where(low, o[:, 0], o[:, 1]) + swap_halves(jnp.where(low, o[:, 1], o[:, 0]))


def kernel(
    ncol, tab, pat, rhs, anc, ids, dinv, panels, sol_out, bu_out,
    idr, arrv, arr,
    stage, ph, pt, dv, dh, dt, pv, p0, rsend, rs, asend, ar, own, sol, out, car, cum, fsend, frecv, bsend, bulk, brecv, anct,
    part, rsr, tot, xsend, solr,
    sem_id, sem_stage, sem_dv, sem_p, sem_a, sem_r, sem_ag_s, sem_ag_r, sem_fs, sem_fr, sem_bs, sem_br, sem_rs_s, sem_rs_r, sem_x,
):
    row, col = lax.axis_index("row"), lax.axis_index("col")
    cap = SLOTS // ncol
    right, left = lax.rem(row + 1, NR), lax.rem(row + NR - 1, NR)

    def rowdev(z):
        return {"row": z}

    def at_row(offset):
        return lax.rem(row + offset + 2 * NR, NR)

    barrier = pltpu.get_barrier_semaphore()

    @pl.loop(1, NR)
    def _(k):
        pl.semaphore_signal(barrier, inc=1, device_id=rowdev(lax.rem(row + k, NR)), device_id_type=pl.DeviceIdType.MESH)

    @pl.loop(1, ncol)
    def _(k):
        pl.semaphore_signal(barrier, inc=1, device_id={"col": lax.rem(col + k, ncol)}, device_id_type=pl.DeviceIdType.MESH)

    def load_panels(l):
        place = (0, 0, 1, 1)[l]
        return pltpu.make_async_copy(panels.at[l], stage.at[place], sem_stage.at[place])

    load_panels(0).start()
    load_panels(3).start()
    pl.semaphore_wait(barrier, NR - 1 + ncol - 1)

    def out_at(l, g, a, b):
        if l < 2:
            return out.at[l, g, pl.ds(a, b - a)]
        return stage.at[0, pl.ds(a, b - a), g, pl.ds(8 * (l - 2), 8)]

    def car_at(l, g, a, b):
        if l == 1:
            return car.at[g, pl.ds(a, b - a)]
        return stage.at[1, pl.ds(a, b - a), g, pl.ds(8 * (l - 2), 8)]

    def row_send(src, dst, send_sem, recv_sem):
        for k in (4, 3, 5, 2, 6, 1, 7):
            z = lax.rem(row + k, NR)
            pltpu.make_async_remote_copy(
                src_ref=src(z), dst_ref=dst(row), send_sem=send_sem, recv_sem=recv_sem,
                device_id=rowdev(z), device_id_type=pl.DeviceIdType.MESH,
            ).start()

    def wait_bytes(ref, sem):
        pltpu.make_async_copy(ref, ref, sem).wait()

    def dinv_send(l):
        row_send(lambda z: dinv.at[l, pl.ds(z * OWN, OWN)], lambda o: dv.at[l, o], sem_dv.at[0, l], sem_dv.at[1, l])
        pltpu.make_async_copy(dinv.at[l, pl.ds(row * OWN, OWN)], dv.at[l, row], sem_dv.at[2, l]).start()

    def dinv_wait(l):
        wait_bytes(dv.at[l, pl.ds(0, NR - 1)], sem_dv.at[0, l])
        wait_bytes(dv.at[l, pl.ds(0, NR - 1)], sem_dv.at[1, l])
        wait_bytes(dv.at[l, 0], sem_dv.at[2, l])
        for j in range(OWN):
            whole = dv[l, :, j].reshape(128, 128)
            dh[l, j] = store_matrix(whole)
            dt[l, j] = store_matrix(whole.T)

    def p0_send(l):
        row_send(lambda z: panels.at[l, 0, pl.ds(z * OWN, OWN)], lambda o: pv.at[l, o], sem_p.at[0, l], sem_p.at[1, l])
        pltpu.make_async_copy(panels.at[l, 0, pl.ds(row * OWN, OWN)], pv.at[l, row], sem_p.at[2, l]).start()

    def p0_wait(l):
        wait_bytes(pv.at[l, pl.ds(0, NR - 1)], sem_p.at[0, l])
        wait_bytes(pv.at[l, pl.ds(0, NR - 1)], sem_p.at[1, l])
        wait_bytes(pv.at[l, 0], sem_p.at[2, l])
        for j in range(OWN):
            p0[l, j] = store_matrix(pv[l, :, j].reshape(128, 128).T)

    def a_send(l):
        col_wait(brecv[l][0], sem_br.at[l, 0])
        col_wait(bwd_buffer(l, 0), sem_bs.at[l, 0])

        @pl.loop(0, SUP, unroll=4)
        def _(k):
            asend[l, k // OWN, k % OWN] = brecv[l][0][tab[l, POS, k], 0]
        ar[l, row] = asend[l, row]
        row_send(lambda z: asend.at[l, z], lambda o: ar.at[l, o], sem_a.at[0, l], sem_a.at[1, l])

    def a_wait(l):
        wait_bytes(ar.at[l, pl.ds(0, NR - 1)], sem_a.at[1, l])
        wait_bytes(ar.at[l, pl.ds(0, NR - 1)], sem_a.at[0, l])

    def r_send(l):
        rs[l, row] = rsend[l, row]
        for h in range(2):
            part_h = pl.ds(2 * h, 2)
            row_send(
                lambda z: rsend.at[l, z, part_h], lambda o: rs.at[l, o, part_h], sem_r.at[0, l, h], sem_r.at[1, l, h]
            )

    def r_wait(l, h):
        wait_bytes(rs.at[l, pl.ds(0, NR - 1), pl.ds(2 * h, 2)], sem_r.at[1, l, h])

    def r_wait_sent(l):
        for h in range(2):
            wait_bytes(rs.at[l, pl.ds(0, NR - 1), pl.ds(2 * h, 2)], sem_r.at[0, l, h])

    def col_send(src, dst, send_sem, recv_sem, pack):
        for i in range(cap):
            pack(src, dst, col * cap + i)
        dst[pl.ds(col * cap, cap)] = src[pl.ds(col * cap, cap)]

        def one(c):
            for i in range(cap):
                pack(src, dst, c * cap + i)
            pltpu.make_async_remote_copy(
                src_ref=src.at[pl.ds(c * cap, cap)], dst_ref=dst.at[pl.ds(col * cap, cap)],
                send_sem=send_sem, recv_sem=recv_sem,
                device_id={"col": c}, device_id_type=pl.DeviceIdType.MESH,
            ).start()

        if ncol == 32:
            x, y, core = col // 8, lax.rem(col // 2, 4), lax.rem(col, 2)

            @pl.loop(1, 16, unroll=3)
            def _(k):
                chip = lax.rem(x + k, 4) * 8 + lax.rem(y + k + k // 4, 4) * 2
                one(chip + core)
                one(chip + 1 - core)
            one(col + 1 - 2 * core)
        else:
            @pl.loop(1, ncol)
            def _(k):
                one(lax.rem(col + k, ncol))

    def col_wait(dst, sem):
        wait_bytes(dst.at[pl.ds(0, SLOTS - cap)], sem)

    def fwd_pack_send(l, g):
        a, b = FWD_GROUPS[g]
        src, dst = fsend[g], frecv[g].at[l % 2]

        def pack(src, dst, s):
            k = tab[l, FSRC, s]
            if l == 0:
                src[s] = out_at(l, k, a, b)[...]
            else:
                src[s] = out_at(l, k, a, b)[...] + car_at(l, k, a, b)[...]
        col_send(src, dst, sem_fs.at[l, g], sem_fr.at[l, g], pack)

    def fwd_collect(l, g):
        a, b = FWD_GROUPS[g]
        dst = frecv[g].at[l % 2]
        col_wait(dst, sem_fr.at[l, g])
        col_wait(fsend[g], sem_fs.at[l, g])

        @pl.loop(0, SLOTS, unroll=4)
        def _(s):
            cum[s, pl.ds(0, b - a)] = dst[s] + cum[arr[3 * l + PREV, s], pl.ds(0, b - a)]

        if g == 0:
            @pl.loop(0, SUP, unroll=4)
            def _(p):
                rsend[l + 1, p // OWN, p % OWN] = rhs[l + 1, p] - cum[arr[3 * l + LAST, p], 0]
        else:
            @pl.loop(0, SUP, unroll=4)
            def _(p):
                car_at(l + 1, p, a - 1, b - 1)[...] = cum[arr[3 * l + LAST, p], pl.ds(0, b - a)]

    def bwd_buffer(l, g):
        a, b = BWD_GROUPS[l][g]
        if b - a == 1 and g < 3:
            return bsend.at[l, g]
        return bulk.at[:, pl.ds(a - (3, 2, 1)[l], b - a)]

    def bwd_pack_send(l, g, source):
        src, dst = bwd_buffer(l, g), brecv[l][g]

        def pack(src, dst, s):
            src[s] = source(arr[3 * l + BSRC, s])
        col_send(src, dst, sem_bs.at[l, g], sem_br.at[l, g], pack)

    def bwd_gather(l, g):
        a, b = BWD_GROUPS[l][g]
        dst = brecv[l][g]
        col_wait(dst, sem_br.at[l, g])
        col_wait(bwd_buffer(l, g), sem_bs.at[l, g])

        @pl.loop(0, SUP, unroll=4)
        def _(k):
            anct[l, k, pl.ds(a, b - a)] = dst[tab[l, POS, k]]

    def ids_send():
        idr[col] = ids[col]

        @pl.loop(1, ncol)
        def _(k):
            c = lax.rem(col + k, ncol)
            pltpu.make_async_remote_copy(
                src_ref=ids.at[c], dst_ref=idr.at[col], send_sem=sem_id.at[0], recv_sem=sem_id.at[1],
                device_id={"col": c}, device_id_type=pl.DeviceIdType.MESH,
            ).start()

    def ids_wait():
        wait_bytes(idr.at[pl.ds(0, ncol - 1)], sem_id.at[1])
        wait_bytes(idr.at[pl.ds(0, ncol - 1)], sem_id.at[0])
        lane = lax.broadcasted_iota(jnp.int32, (8, 128), 1)
        odd = lax.rem(lax.broadcasted_iota(jnp.int32, (8, 128), 0), 2)
        mine = lax.rem(lane, 2) == odd
        zero = jnp.zeros((8, 128), jnp.int32)
        half = zero
        for c in range(32):
            half = half + jnp.where(mine & (lane // 2 == c), idr[c], zero)
        every = half + jnp.where(odd == 0, pltpu.roll(half, 7, 0), pltpu.roll(half, 1, 0))
        prev, last = zero - 1, zero - 1
        for c in range(32):
            tile, slot = idr[c], odd + 2 * c
            prev = jnp.maximum(prev, jnp.where((tile == every) & (slot < lane), slot, -1))
            last = jnp.maximum(last, jnp.where(tile == lane + 1, slot, -1))
        prev = jnp.maximum(prev, jnp.where(odd == 0, pltpu.roll(prev, 7, 0), pltpu.roll(prev, 1, 0)))
        last = jnp.maximum(last, jnp.where(odd == 0, pltpu.roll(last, 7, 0), pltpu.roll(last, 1, 0)))
        prev = jnp.where(prev < 0, SLOTS, prev)
        last = jnp.where(last < 0, SLOTS, last)
        source = jnp.maximum(every - 1, 0)
        for l in range(3):
            for kind, value in ((PREV, prev), (LAST, last), (BSRC, source)):
                arrv[3 * l + kind : 3 * l + kind + 1, :] = value[2 * l : 2 * l + 1, :]
        copy = pltpu.make_async_copy(arrv, arr, sem_id.at[2])
        copy.start()
        copy.wait()

    def convert(l, low=0, high=SUP):
        place = (0, 0, 1, 1)[l]
        if low == 0:
            load_panels(l).wait()

        @pl.loop(low, high, unroll=2)
        def _(g):
            blocks = [stage[place, 0, g]]
            for d in range(1, ANC):
                blocks.append(stage[place, d, g] * pat[l, d - 1, g].astype(F32))
            whole = jnp.concatenate(blocks, axis=0)
            ph[l, g] = store_matrix(whole)
            pt[l, g] = store_matrix(whole.T)
        if l in (0, 3) and high == SUP:
            load_panels((1, None, None, 2)[l]).start()

    def ag_copy(l, c, t, way):
        origin = at_row(1 - t) if way == 0 else at_row(t - 1)
        return pltpu.make_async_remote_copy(
            src_ref=sol.at[l % 2, origin, c], dst_ref=sol.at[l % 2, origin, c],
            send_sem=sem_ag_s.at[l, c, t - 1, way], recv_sem=sem_ag_r.at[l, c, t - 1, way],
            device_id=rowdev(right if way == 0 else left), device_id_type=pl.DeviceIdType.MESH,
        )

    def ag_ways(c, t):
        return (0, 1) if t < 4 else (c % 2,)

    def product(l, g):
        out_at(l, g, 0, 8)[...] = multiply(ph[l, g], sol[l % 2, g // OWN, g % OWN].reshape(8, 8, 128))

    def solve(l):
        for c in range(OWN):
            if c % 2 == 0:
                r_wait(l, c // 2)
            own[l, c] = multiply(dh[l, c], rs[l, :, c]).reshape(64, 128)
            sol[l % 2, row, c] = own[l, c]
            for way in ag_ways(c, 1):
                ag_copy(l, c, 1, way).start()
        r_wait_sent(l)

    def spread_step(l, t):
        if t == 0:
            for c in range(OWN):
                product(l, row * OWN + c)
            return
        for c in range(OWN):
            for way in ag_ways(c, t):
                ag_copy(l, c, t, way).wait_recv()
                if t < 4 and way in ag_ways(c, t + 1):
                    ag_copy(l, c, t + 1, way).start()
            for offset in (4,) if t == 4 else (-t, t):
                product(l, at_row(offset) * OWN + c)
        if t == 4:
            for t in range(1, 5):
                for c in range(OWN):
                    for way in ag_ways(c, t):
                        ag_copy(l, c, t, way).wait_send()

    def spread_solved(l, extra=None):
        for t in range(5):
            spread_step(l, t)
            if extra is not None and t < 4:
                extra(t)

    def rs_dest(t, way):
        return at_row(5 - t) if way == 0 else at_row(t - 5)

    def rs_ways(c, t):
        return (0, 1) if t > 1 else (c % 2,)

    def rs_copy(l, c, t, way):
        first = t == 1 or way not in rs_ways(c, t - 1)
        src = part.at[l % 2, rs_dest(t, way), c] if first else rsr.at[l % 2, way, t - 2, c]
        return pltpu.make_async_remote_copy(
            src_ref=src, dst_ref=rsr.at[l % 2, way, t - 1, c],
            send_sem=sem_rs_s.at[l, c, t - 1, way], recv_sem=sem_rs_r.at[l, c, t - 1, way],
            device_id=rowdev(right if way == 0 else left), device_id_type=pl.DeviceIdType.MESH,
        )

    def ring_step(l, t):
        for c in range(OWN):
            for way in rs_ways(c, t):
                if t > 1 and way in rs_ways(c, t - 1):
                    rs_copy(l, c, t - 1, way).wait_recv()
                    rsr[l % 2, way, t - 2, c] += part[l % 2, rs_dest(t, way), c]
                rs_copy(l, c, t, way).start()

    def ring_end(l):
        for c in range(OWN):
            for way in (0, 1):
                rs_copy(l, c, 4, way).wait_recv()
            tot[c] = part[l % 2, row, c] + rsr[l % 2, 0, 3, c] + rsr[l % 2, 1, 3, c]
        for c in range(OWN):
            for t in range(1, 5):
                for way in rs_ways(c, t):
                    rs_copy(l, c, t, way).wait_send()

    def partial_sums(l, low, high):
        @pl.loop(low, high, unroll=4)
        def _(g):
            part[l % 2, g // OWN, g % OWN] = multiply(pt[l, g], anc[g] if l == 3 else anct[l, g]).reshape(64, 128)

    def finish(l, c):
        reduced = (own[l, c] - tot[c]).reshape(8, 8, 128)
        if l < 3:
            reduced = reduced - multiply(p0[l, c], ar[l, :, c])
        xsend[l, :, c] = multiply(dt[l, c], reduced)
        if c % 2 == 1:
            h = c // 2
            part_h = pl.ds(2 * h, 2)
            solr[l, row, part_h] = xsend[l, row, part_h]
            row_send(
                lambda z: xsend.at[l, z, part_h], lambda o: solr.at[l, o, part_h], sem_x.at[0, l, h], sem_x.at[1, l, h]
            )

    def finish_wait(l):
        for h in range(2):
            for k in (1, 0):
                wait_bytes(solr.at[l, pl.ds(0, NR - 1), pl.ds(2 * h, 2)], sem_x.at[k, l, h])

    def emit(l):
        sol_out[l] = solr[l].reshape(SUP, 8, 128)

    def finish_all(l):
        for c in range(OWN):
            finish(l, c)

    def send_down(l):
        bwd_pack_send(l, 0, lambda k: solr[l + 1, k // OWN, pl.ds(k % OWN, 1)])

    def beside(l, t):
        if l == 0:
            if t < 2:
                convert(1, 16 * t, 16 * t + 16)
            else:
                partial_sums(3, 16 * t - 32, 16 * t - 16)
        elif l == 1:
            if t < 2:
                convert(2, 16 * t, 16 * t + 16)
            elif t == 2:
                ring_step(3, 2)
                fwd_collect(0, 1)
            else:
                fwd_collect(0, 2)

                @pl.loop(0, SUP)
                def _(g):
                    car_at(2, g, 7, 8)[...] = jnp.zeros((1, 8, 128), F32)
        else:
            if t < 2:
                partial_sums(2, 16 * t, 16 * t + 16)
            elif t == 2:
                fwd_collect(1, 1)
            else:
                fwd_collect(1, 2)

    def relay(l, g):
        a, b = BWD_GROUPS[l][g]
        bwd_pack_send(l, g, lambda k: anct[l + 1, k, pl.ds(a - 1, b - a)])

    rsend[0] = rhs[0].reshape(NR, OWN, 8, 128)
    r_send(0)
    dinv_send(0)
    cum[SLOTS] = jnp.zeros(cum.shape[1:], F32)
    ids_send()
    for r in range(9, 16):
        arrv[r : r + 1, :] = jnp.zeros((1, 128), jnp.int32)

    @pl.loop(0, SUP)
    def _(g):
        car[g, 7] = jnp.zeros((8, 128), F32)
        for l in range(3):
            anct[l, g, 0] = jnp.zeros((8, 128), F32)
    convert(0)
    ids_wait()
    bwd_pack_send(2, 1, lambda k: anc[k, pl.ds(0, 7)])
    convert(3)
    dinv_wait(0)
    for l in range(LEVELS - 1):
        solve(l)
        spread_solved(l, functools.partial(beside, l))
        fwd_pack_send(l, 0)
        dinv_send(l + 1)
        ring_step(3, (1, 3, 4)[l])
        fwd_pack_send(l, 1)
        fwd_collect(l, 0)
        r_send(l + 1)
        p0_send(l)
        if l == 0:
            fwd_pack_send(0, 2)
            fwd_pack_send(0, 3)
            bwd_gather(2, 1)
            relay(1, 2)
            fwd_pack_send(0, 4)
        if l == 1:
            fwd_collect(0, 3)
            fwd_pack_send(1, 2)
            fwd_collect(0, 4)
            fwd_pack_send(1, 3)
            relay(1, 3)
            relay(1, 4)
        if l == 2:
            bwd_gather(1, 2)
            relay(0, 3)
        dinv_wait(l + 1)

    ring_step(2, 1)
    ring_end(3)
    solve(3)
    finish_all(3)
    bwd_gather(1, 3)
    relay(0, 4)
    ring_step(2, 2)
    p0_wait(2)
    finish_wait(3)
    send_down(2)
    fwd_pack_send(0, 5)
    ring_step(2, 3)
    spread_step(3, 0)
    p0_wait(1)
    emit(3)
    spread_step(3, 1)

    a_send(2)
    bwd_pack_send(1, 1, lambda k: asend[2, k // OWN, pl.ds(k % OWN, 1)])
    bwd_gather(1, 4)
    relay(0, 5)
    ring_step(2, 4)
    spread_step(3, 2)
    ring_end(2)
    a_wait(2)
    finish_all(2)
    p0_wait(0)
    fwd_collect(0, 5)
    fwd_pack_send(1, 4)
    bwd_gather(1, 1)
    partial_sums(1, 0, SUP)
    ring_step(1, 1)
    finish_wait(2)
    send_down(1)
    fwd_pack_send(1, 5)
    ring_step(1, 2)
    emit(2)
    ring_step(1, 3)

    a_send(1)
    bwd_pack_send(0, 1, lambda k: asend[1, k // OWN, pl.ds(k % OWN, 1)])
    relay(0, 2)
    fwd_collect(1, 3)
    fwd_pack_send(2, 2)
    ring_step(1, 4)
    bwd_gather(0, 3)
    bwd_gather(0, 4)
    ring_end(1)
    a_wait(1)
    finish_all(1)
    bwd_gather(0, 5)
    bwd_gather(0, 1)
    bwd_gather(0, 2)
    partial_sums(0, 0, SUP)
    ring_step(0, 1)
    finish_wait(1)
    send_down(0)
    fwd_collect(1, 4)
    fwd_pack_send(2, 3)
    ring_step(0, 2)
    fwd_collect(1, 5)
    fwd_pack_send(2, 4)
    fwd_pack_send(2, 5)
    emit(1)
    ring_step(0, 3)

    a_send(0)
    ring_step(0, 4)
    spread_step(3, 3)
    ring_end(0)
    a_wait(0)
    finish_all(0)
    spread_step(3, 4)
    for g in range(1, 6):
        fwd_collect(2, g)

    @pl.loop(0, SUP)
    def _(g):
        bu_out[g, pl.ds(0, 7)] = out_at(3, g, 0, 7)[...] + car_at(3, g, 0, 7)[...]
        bu_out[g, pl.ds(7, 1)] = out_at(3, g, 7, 8)[...]
    finish_wait(0)
    emit(0)


def tables(parent_owner, parent_local, ncol):
    cap = SLOTS // ncol
    owner = parent_owner[:, :, 0]
    here = jnp.arange(SUP, dtype=jnp.int32)
    same = (owner[:, :, None] == owner[:, None, :]) & (here[None, :, None] < here[None, None, :])
    pos = owner * cap + jnp.sum(same.astype(jnp.int32), axis=1)
    slots = jnp.arange(SLOTS, dtype=jnp.int32)
    hit = pos[:, None, :] == slots[None, :, None]
    fsrc = jnp.sum(jnp.where(hit, here[None, None, :], 0), axis=2)
    ids = jnp.sum(jnp.where(hit, parent_local[:, None, :] + 1, 0), axis=2)
    ids = ids.reshape(3, ncol, cap).transpose(1, 0, 2).reshape(ncol, 3 * cap)
    ids = jnp.pad(ids, ((0, 0), (0, 8 - 3 * cap)))
    ids = jnp.broadcast_to(ids[:, :, None], (ncol, 8, 128))
    wide = lambda x: jnp.pad(x, ((0, 0), (0, SLOTS - x.shape[1])))
    return jnp.stack([fsrc, wide(pos)], axis=1), ids


def per_device(ncol, rhs, dinv, panels, pattern, parent_owner, parent_local, ancestor_solution):
    tab, ids = tables(parent_owner, parent_local, ncol)
    rhs_p = rhs.reshape(LEVELS, 2, 8, SUP, 64).transpose(0, 3, 2, 1, 4).reshape(LEVELS, SUP, 8, 128)
    anc_p = ancestor_solution.reshape(2, 8, SUP, ANC, 64).transpose(2, 3, 1, 0, 4).reshape(SUP, ANC, 8, 128)
    vmem = pl.BlockSpec(memory_space=pltpu.VMEM)
    smem = pl.BlockSpec(memory_space=pltpu.SMEM)
    anywhere = pl.BlockSpec(memory_space=pl.ANY)
    sems = pltpu.SemaphoreType.DMA
    tile = (8, 128)
    fsend = tuple(pltpu.VMEM((SLOTS, b - a) + tile, F32) for a, b in FWD_GROUPS)
    frecv = tuple(pltpu.VMEM((2, SLOTS, b - a) + tile, F32) for a, b in FWD_GROUPS)
    bbuf = tuple(tuple(pltpu.VMEM((SLOTS, b - a) + tile, F32) for a, b in groups) for groups in BWD_GROUPS)
    sol, bu = pl.pallas_call(
        functools.partial(kernel, ncol),
        out_shape=(
            jax.ShapeDtypeStruct((LEVELS, SUP) + tile, F32),
            jax.ShapeDtypeStruct((SUP, ANC) + tile, F32),
        ),
        in_specs=[smem, smem, vmem, vmem, vmem, anywhere, anywhere],
        out_specs=(vmem, vmem),
        scratch_shapes=[
            pltpu.VMEM((32,) + tile, jnp.int32),
            pltpu.VMEM((16, 128), jnp.int32),
            pltpu.SMEM((16, 128), jnp.int32),
            pltpu.VMEM((2, ANC, SUP, 16, 128), F32),
            pltpu.VMEM((LEVELS, SUP, 128, 256), BF16),
            pltpu.VMEM((LEVELS, SUP, 128, 256), BF16),
            pltpu.VMEM((LEVELS, NR, OWN, 16, 128), F32),
            pltpu.VMEM((LEVELS, OWN, 128, 256), BF16),
            pltpu.VMEM((LEVELS, OWN, 128, 256), BF16),
            pltpu.VMEM((3, NR, OWN, 16, 128), F32),
            pltpu.VMEM((3, OWN, 128, 256), BF16),
            pltpu.VMEM((LEVELS, NR, OWN) + tile, F32),
            pltpu.VMEM((LEVELS, NR, OWN) + tile, F32),
            pltpu.VMEM((3, NR, OWN) + tile, F32),
            pltpu.VMEM((3, NR, OWN) + tile, F32),
            pltpu.VMEM((LEVELS, OWN, 64, 128), F32),
            pltpu.VMEM((2, NR, OWN, 64, 128), F32),
            pltpu.VMEM((2, SUP, ANC) + tile, F32),
            pltpu.VMEM((SUP, ANC) + tile, F32),
            pltpu.VMEM((SLOTS + 1, 2) + tile, F32),
            fsend, frecv, pltpu.VMEM((3, 3, SLOTS, 1) + tile, F32), pltpu.VMEM((SLOTS, 7) + tile, F32), bbuf,
            pltpu.VMEM((3, SUP, ANC) + tile, F32),
            pltpu.VMEM((2, NR, OWN, 64, 128), F32),
            pltpu.VMEM((2, 2, 4, OWN, 64, 128), F32),
            pltpu.VMEM((OWN, 64, 128), F32),
            pltpu.VMEM((LEVELS, NR, OWN) + tile, F32),
            pltpu.VMEM((LEVELS, NR, OWN) + tile, F32),
            sems((3,)), sems((2,)), sems((3, LEVELS)), sems((3, 3)), sems((2, 3)), sems((2, LEVELS, 2)),
            sems((LEVELS, OWN, 4, 2)), sems((LEVELS, OWN, 4, 2)),
            sems((3, 6)), sems((3, 6)), sems((3, 6)), sems((3, 6)),
            sems((LEVELS, OWN, 4, 2)), sems((LEVELS, OWN, 4, 2)), sems((2, LEVELS, 2)),
        ],
        compiler_params=pltpu.CompilerParams(
            collective_id=0, has_side_effects=True, vmem_limit_bytes=60 * 1024 * 1024
        ),
        cost_estimate=pl.CostEstimate(flops=4 * 10**9, bytes_accessed=12 * 10**6, transcendentals=0),
    )(tab, pattern, rhs_p, anc_p, ids, dinv, panels)
    solution = sol.reshape(LEVELS, SUP, 8, 2, 64).transpose(0, 3, 2, 1, 4).reshape(LEVELS, 16, SUP, 64)
    boundary = bu.reshape(SUP, ANC, 8, 2, 64).transpose(3, 2, 0, 1, 4).reshape(16, SUP, ANC, 64)
    return solution, boundary


def solution(mesh):
    placed = (
        P(None, "row", "col", None),
        P(None, "col", "row", None),
        P(None, None, "col", "row", None),
        P(None, None, "col"),
        P(None, "col", None),
        P(None, "col"),
        P("row", "col", None, None),
    )
    return jax.shard_map(
        functools.partial(per_device, mesh.shape["col"]),
        mesh=mesh,
        in_specs=placed,
        out_specs=(P(None, "row", "col", None), P("row", "col", None, None)),
        check_vma=False,
    )
```

```python
import functools

import jax
import jax.numpy as jnp
from jax import lax
from jax.experimental import pallas as pl
from jax.experimental.pallas import tpu as pltpu
from jax.sharding import PartitionSpec as P

F32 = jnp.float32
BF16 = jnp.bfloat16
LEVELS = 4
ANC = 8
SUP = 32
SLOTS = 64
NR = 8
OWN = SUP // NR
FWD_GROUPS = ((0, 1), (1, 2), (2, 3), (3, 4), (4, 6), (6, 8))
BWD_GROUPS = (
    ((0, 1), (1, 2), (2, 3), (3, 5), (5, 7), (7, 8)),
    ((0, 1), (1, 2), (2, 4), (4, 6), (6, 8)),
    ((0, 1), (1, 8)),
)
FSRC, POS = range(2)
PREV, LAST, BSRC = range(3)


def low_lanes(shape):
    return lax.broadcasted_iota(jnp.int32, shape, len(shape) - 1) < 64


def swap_halves(x):
    return pltpu.roll(x.reshape(-1, 128), 64, 1).reshape(x.shape)


def split(x):
    high = x.astype(BF16).astype(F32)
    return high, x - high


def store_matrix(block):
    high, low = split(block)
    return jnp.concatenate([high.astype(BF16), low.astype(BF16)], axis=1)


def multiply(matrix, tiles):
    low = low_lanes((8, 128))
    high, rest = split(tiles)
    high_r, rest_r = swap_halves(high), swap_halves(rest)
    rows = []
    for z in range(8):
        rows += [jnp.where(low, high[z], rest_r[z]), jnp.where(low, high_r[z], rest[z])]
    weights = jnp.concatenate(rows, axis=0).astype(BF16)
    weights = jnp.concatenate([weights, weights], axis=0)
    o = jnp.dot(matrix, weights, preferred_element_type=F32).reshape(8, 2, 8, 128)
    low = low_lanes((8, 8, 128))
    return jnp.where(low, o[:, 0], o[:, 1]) + swap_halves(jnp.where(low, o[:, 1], o[:, 0]))


def kernel(
    ncol, tab, pat, ids, rhs_whole, anc_whole, dinv, panels, sol_out, bu_out,
    rhs, anc, rhs_near, anc_near, sem_near, idr, arrv, arr,
    stage, ph, pt, dv, dh, dt, pv, p0, rsend, rs, asend, ar, own, sol, out, car, cum, fsend, frecv, bsend, bulk, brecv, anct,
    part, rsr, tot, xsend, solr,
    sem_id, sem_stage, sem_dv, sem_p, sem_a, sem_r, sem_ag_s, sem_ag_r, sem_fs, sem_fr, sem_bs, sem_br, sem_rs_s, sem_rs_r, sem_x,
):
    row, col = lax.axis_index("row"), lax.axis_index("col")
    cap = SLOTS // ncol
    right, left = lax.rem(row + 1, NR), lax.rem(row + NR - 1, NR)

    def rowdev(z):
        return {"row": z}

    def at_row(offset):
        return lax.rem(row + offset + 2 * NR, NR)

    barrier = pltpu.get_barrier_semaphore()

    @pl.loop(1, NR)
    def _(k):
        pl.semaphore_signal(barrier, inc=1, device_id=rowdev(lax.rem(row + k, NR)), device_id_type=pl.DeviceIdType.MESH)

    @pl.loop(1, ncol)
    def _(k):
        pl.semaphore_signal(barrier, inc=1, device_id={"col": lax.rem(col + k, ncol)}, device_id_type=pl.DeviceIdType.MESH)

    def load_panels(l):
        place = (0, 0, 1, 1)[l]
        return pltpu.make_async_copy(panels.at[l], stage.at[place], sem_stage.at[place])

    def load_rhs(l):
        return pltpu.make_async_copy(rhs_whole.at[l], rhs_near.at[l % 2], sem_near.at[0, l % 2])

    def load_anc(b):
        return pltpu.make_async_copy(anc_whole.at[:, pl.ds(8 * b, 8)], anc_near.at[b % 2], sem_near.at[1, b % 2])

    def pack_rows(x):
        return jnp.swapaxes(jnp.concatenate([x[:8], x[8:]], axis=2), 0, 1)

    def pack_rhs(l):
        load_rhs(l).wait()
        for b in range(SUP // 8):
            rhs[l, 8 * b : 8 * b + 8] = pack_rows(rhs_near[l % 2, :, 8 * b : 8 * b + 8])
        if l + 2 < LEVELS:
            load_rhs(l + 2).start()

    def pack_anc(b):
        load_anc(b).wait()

        @pl.loop(0, 8, unroll=2)
        def _(g):
            anc[8 * b + g] = pack_rows(anc_near[b % 2, :, g])
        if b + 2 < SUP // 8:
            load_anc(b + 2).start()

    for k in range(2):
        load_rhs(k).start()
        load_anc(k).start()
    load_panels(0).start()
    load_panels(3).start()
    pl.semaphore_wait(barrier, NR - 1 + ncol - 1)

    def out_at(l, g, a, b):
        if l < 2:
            return out.at[l, g, pl.ds(a, b - a)]
        return stage.at[0, pl.ds(a, b - a), g, pl.ds(8 * (l - 2), 8)]

    def car_at(l, g, a, b):
        if l == 1:
            return car.at[g, pl.ds(a, b - a)]
        return stage.at[1, pl.ds(a, b - a), g, pl.ds(8 * (l - 2), 8)]

    def row_send(src, dst, send_sem, recv_sem):
        for k in (4, 3, 5, 2, 6, 1, 7):
            z = lax.rem(row + k, NR)
            pltpu.make_async_remote_copy(
                src_ref=src(z), dst_ref=dst(row), send_sem=send_sem, recv_sem=recv_sem,
                device_id=rowdev(z), device_id_type=pl.DeviceIdType.MESH,
            ).start()

    def wait_bytes(ref, sem):
        pltpu.make_async_copy(ref, ref, sem).wait()

    def dinv_send(l):
        row_send(lambda z: dinv.at[l, pl.ds(z * OWN, OWN)], lambda o: dv.at[l, o], sem_dv.at[0, l], sem_dv.at[1, l])
        pltpu.make_async_copy(dinv.at[l, pl.ds(row * OWN, OWN)], dv.at[l, row], sem_dv.at[2, l]).start()

    def dinv_wait(l):
        wait_bytes(dv.at[l, pl.ds(0, NR - 1)], sem_dv.at[0, l])
        wait_bytes(dv.at[l, pl.ds(0, NR - 1)], sem_dv.at[1, l])
        wait_bytes(dv.at[l, 0], sem_dv.at[2, l])
        for j in range(OWN):
            whole = dv[l, :, j].reshape(128, 128)
            dh[l, j] = store_matrix(whole)
            dt[l, j] = store_matrix(whole.T)

    def p0_send(l):
        row_send(lambda z: panels.at[l, 0, pl.ds(z * OWN, OWN)], lambda o: pv.at[l, o], sem_p.at[0, l], sem_p.at[1, l])
        pltpu.make_async_copy(panels.at[l, 0, pl.ds(row * OWN, OWN)], pv.at[l, row], sem_p.at[2, l]).start()

    def p0_wait(l):
        wait_bytes(pv.at[l, pl.ds(0, NR - 1)], sem_p.at[0, l])
        wait_bytes(pv.at[l, pl.ds(0, NR - 1)], sem_p.at[1, l])
        wait_bytes(pv.at[l, 0], sem_p.at[2, l])
        for j in range(OWN):
            p0[l, j] = store_matrix(pv[l, :, j].reshape(128, 128).T)

    def a_send(l):
        col_wait(brecv[l][0], sem_br.at[l, 0])
        col_wait(bwd_buffer(l, 0), sem_bs.at[l, 0])

        @pl.loop(0, SUP, unroll=4)
        def _(k):
            asend[l, k // OWN, k % OWN] = brecv[l][0][tab[l, POS, k], 0]
        ar[l, row] = asend[l, row]
        row_send(lambda z: asend.at[l, z], lambda o: ar.at[l, o], sem_a.at[0, l], sem_a.at[1, l])

    def a_wait(l):
        wait_bytes(ar.at[l, pl.ds(0, NR - 1)], sem_a.at[1, l])
        wait_bytes(ar.at[l, pl.ds(0, NR - 1)], sem_a.at[0, l])

    def r_send(l):
        rs[l, row] = rsend[l, row]
        for h in range(2):
            part_h = pl.ds(2 * h, 2)
            row_send(
                lambda z: rsend.at[l, z, part_h], lambda o: rs.at[l, o, part_h], sem_r.at[0, l, h], sem_r.at[1, l, h]
            )

    def r_wait(l, h):
        wait_bytes(rs.at[l, pl.ds(0, NR - 1), pl.ds(2 * h, 2)], sem_r.at[1, l, h])

    def r_wait_sent(l):
        for h in range(2):
            wait_bytes(rs.at[l, pl.ds(0, NR - 1), pl.ds(2 * h, 2)], sem_r.at[0, l, h])

    def col_send(src, dst, send_sem, recv_sem, pack):
        for i in range(cap):
            pack(src, dst, col * cap + i)
        dst[pl.ds(col * cap, cap)] = src[pl.ds(col * cap, cap)]

        def one(c):
            for i in range(cap):
                pack(src, dst, c * cap + i)
            pltpu.make_async_remote_copy(
                src_ref=src.at[pl.ds(c * cap, cap)], dst_ref=dst.at[pl.ds(col * cap, cap)],
                send_sem=send_sem, recv_sem=recv_sem,
                device_id={"col": c}, device_id_type=pl.DeviceIdType.MESH,
            ).start()

        if ncol == 32:
            x, y, core = col // 8, lax.rem(col // 2, 4), lax.rem(col, 2)

            @pl.loop(1, 16, unroll=3)
            def _(k):
                chip = lax.rem(x + k, 4) * 8 + lax.rem(y + k + k // 4, 4) * 2
                one(chip + core)
                one(chip + 1 - core)
            one(col + 1 - 2 * core)
        else:
            @pl.loop(1, ncol)
            def _(k):
                one(lax.rem(col + k, ncol))

    def col_wait(dst, sem):
        wait_bytes(dst.at[pl.ds(0, SLOTS - cap)], sem)

    def fwd_pack_send(l, g):
        a, b = FWD_GROUPS[g]
        src, dst = fsend[g], frecv[g].at[l % 2]

        def pack(src, dst, s):
            k = tab[l, FSRC, s]
            if l == 0:
                src[s] = out_at(l, k, a, b)[...]
            else:
                src[s] = out_at(l, k, a, b)[...] + car_at(l, k, a, b)[...]
        col_send(src, dst, sem_fs.at[l, g], sem_fr.at[l, g], pack)

    def fwd_collect(l, g):
        a, b = FWD_GROUPS[g]
        dst = frecv[g].at[l % 2]
        col_wait(dst, sem_fr.at[l, g])
        col_wait(fsend[g], sem_fs.at[l, g])

        @pl.loop(0, SLOTS, unroll=4)
        def _(s):
            cum[s, pl.ds(0, b - a)] = dst[s] + cum[arr[3 * l + PREV, s], pl.ds(0, b - a)]

        if g == 0:
            @pl.loop(0, SUP, unroll=4)
            def _(p):
                rsend[l + 1, p // OWN, p % OWN] = rhs[l + 1, p] - cum[arr[3 * l + LAST, p], 0]
        else:
            @pl.loop(0, SUP, unroll=4)
            def _(p):
                car_at(l + 1, p, a - 1, b - 1)[...] = cum[arr[3 * l + LAST, p], pl.ds(0, b - a)]

    def bwd_buffer(l, g):
        a, b = BWD_GROUPS[l][g]
        if b - a == 1 and g < 3:
            return bsend.at[l, g]
        return bulk.at[:, pl.ds(a - (3, 2, 1)[l], b - a)]

    def bwd_pack_send(l, g, source):
        src, dst = bwd_buffer(l, g), brecv[l][g]

        def pack(src, dst, s):
            src[s] = source(arr[3 * l + BSRC, s])
        col_send(src, dst, sem_bs.at[l, g], sem_br.at[l, g], pack)

    def bwd_gather(l, g):
        a, b = BWD_GROUPS[l][g]
        dst = brecv[l][g]
        col_wait(dst, sem_br.at[l, g])
        col_wait(bwd_buffer(l, g), sem_bs.at[l, g])

        @pl.loop(0, SUP, unroll=4)
        def _(k):
            anct[l, k, pl.ds(a, b - a)] = dst[tab[l, POS, k]]

    def ids_send():
        idr[col] = ids[col]

        @pl.loop(1, ncol)
        def _(k):
            c = lax.rem(col + k, ncol)
            pltpu.make_async_remote_copy(
                src_ref=ids.at[c], dst_ref=idr.at[col], send_sem=sem_id.at[0], recv_sem=sem_id.at[1],
                device_id={"col": c}, device_id_type=pl.DeviceIdType.MESH,
            ).start()

    def ids_wait():
        wait_bytes(idr.at[pl.ds(0, ncol - 1)], sem_id.at[1])
        wait_bytes(idr.at[pl.ds(0, ncol - 1)], sem_id.at[0])
        lane = lax.broadcasted_iota(jnp.int32, (8, 128), 1)
        odd = lax.rem(lax.broadcasted_iota(jnp.int32, (8, 128), 0), 2)
        mine = lax.rem(lane, 2) == odd
        zero = jnp.zeros((8, 128), jnp.int32)
        half = zero
        for c in range(32):
            half = half + jnp.where(mine & (lane // 2 == c), idr[c], zero)
        every = half + jnp.where(odd == 0, pltpu.roll(half, 7, 0), pltpu.roll(half, 1, 0))
        prev, last = zero - 1, zero - 1
        for c in range(32):
            tile, slot = idr[c], odd + 2 * c
            prev = jnp.maximum(prev, jnp.where((tile == every) & (slot < lane), slot, -1))
            last = jnp.maximum(last, jnp.where(tile == lane + 1, slot, -1))
        prev = jnp.maximum(prev, jnp.where(odd == 0, pltpu.roll(prev, 7, 0), pltpu.roll(prev, 1, 0)))
        last = jnp.maximum(last, jnp.where(odd == 0, pltpu.roll(last, 7, 0), pltpu.roll(last, 1, 0)))
        prev = jnp.where(prev < 0, SLOTS, prev)
        last = jnp.where(last < 0, SLOTS, last)
        source = jnp.maximum(every - 1, 0)
        for l in range(3):
            for kind, value in ((PREV, prev), (LAST, last), (BSRC, source)):
                arrv[3 * l + kind : 3 * l + kind + 1, :] = value[2 * l : 2 * l + 1, :]
        copy = pltpu.make_async_copy(arrv, arr, sem_id.at[2])
        copy.start()
        copy.wait()

    def convert(l, low=0, high=SUP):
        place = (0, 0, 1, 1)[l]
        if low == 0:
            load_panels(l).wait()

        @pl.loop(low, high, unroll=2)
        def _(g):
            blocks = [stage[place, 0, g]]
            for d in range(1, ANC):
                blocks.append(stage[place, d, g] * pat[l, d - 1, g].astype(F32))
            whole = jnp.concatenate(blocks, axis=0)
            ph[l, g] = store_matrix(whole)
            pt[l, g] = store_matrix(whole.T)
        if l in (0, 3) and high == SUP:
            load_panels((1, None, None, 2)[l]).start()

    def ag_copy(l, c, t, way):
        origin = at_row(1 - t) if way == 0 else at_row(t - 1)
        return pltpu.make_async_remote_copy(
            src_ref=sol.at[l % 2, origin, c], dst_ref=sol.at[l % 2, origin, c],
            send_sem=sem_ag_s.at[l, c, t - 1, way], recv_sem=sem_ag_r.at[l, c, t - 1, way],
            device_id=rowdev(right if way == 0 else left), device_id_type=pl.DeviceIdType.MESH,
        )

    def ag_ways(c, t):
        return (0, 1) if t < 4 else (c % 2,)

    def product(l, g):
        out_at(l, g, 0, 8)[...] = multiply(ph[l, g], sol[l % 2, g // OWN, g % OWN].reshape(8, 8, 128))

    def solve(l):
        for c in range(OWN):
            if c % 2 == 0:
                r_wait(l, c // 2)
            own[l, c] = multiply(dh[l, c], rs[l, :, c]).reshape(64, 128)
            sol[l % 2, row, c] = own[l, c]
            for way in ag_ways(c, 1):
                ag_copy(l, c, 1, way).start()
        r_wait_sent(l)

    def spread_step(l, t):
        if t == 0:
            for c in range(OWN):
                product(l, row * OWN + c)
            return
        for c in range(OWN):
            for way in ag_ways(c, t):
                ag_copy(l, c, t, way).wait_recv()
                if t < 4 and way in ag_ways(c, t + 1):
                    ag_copy(l, c, t + 1, way).start()
            for offset in (4,) if t == 4 else (-t, t):
                product(l, at_row(offset) * OWN + c)
        if t == 4:
            for t in range(1, 5):
                for c in range(OWN):
                    for way in ag_ways(c, t):
                        ag_copy(l, c, t, way).wait_send()

    def spread_solved(l, extra=None):
        for t in range(5):
            spread_step(l, t)
            if extra is not None and t < 4:
                extra(t)

    def rs_dest(t, way):
        return at_row(5 - t) if way == 0 else at_row(t - 5)

    def rs_ways(c, t):
        return (0, 1) if t > 1 else (c % 2,)

    def rs_copy(l, c, t, way):
        first = t == 1 or way not in rs_ways(c, t - 1)
        src = part.at[l % 2, rs_dest(t, way), c] if first else rsr.at[l % 2, way, t - 2, c]
        return pltpu.make_async_remote_copy(
            src_ref=src, dst_ref=rsr.at[l % 2, way, t - 1, c],
            send_sem=sem_rs_s.at[l, c, t - 1, way], recv_sem=sem_rs_r.at[l, c, t - 1, way],
            device_id=rowdev(right if way == 0 else left), device_id_type=pl.DeviceIdType.MESH,
        )

    def ring_step(l, t):
        for c in range(OWN):
            for way in rs_ways(c, t):
                if t > 1 and way in rs_ways(c, t - 1):
                    rs_copy(l, c, t - 1, way).wait_recv()
                    rsr[l % 2, way, t - 2, c] += part[l % 2, rs_dest(t, way), c]
                rs_copy(l, c, t, way).start()

    def ring_end(l):
        for c in range(OWN):
            for way in (0, 1):
                rs_copy(l, c, 4, way).wait_recv()
            tot[c] = part[l % 2, row, c] + rsr[l % 2, 0, 3, c] + rsr[l % 2, 1, 3, c]
        for c in range(OWN):
            for t in range(1, 5):
                for way in rs_ways(c, t):
                    rs_copy(l, c, t, way).wait_send()

    def partial_sums(l, low, high):
        @pl.loop(low, high, unroll=4)
        def _(g):
            part[l % 2, g // OWN, g % OWN] = multiply(pt[l, g], anc[g] if l == 3 else anct[l, g]).reshape(64, 128)

    def finish(l, c):
        reduced = (own[l, c] - tot[c]).reshape(8, 8, 128)
        if l < 3:
            reduced = reduced - multiply(p0[l, c], ar[l, :, c])
        xsend[l, :, c] = multiply(dt[l, c], reduced)
        if c % 2 == 1:
            h = c // 2
            part_h = pl.ds(2 * h, 2)
            solr[l, row, part_h] = xsend[l, row, part_h]
            row_send(
                lambda z: xsend.at[l, z, part_h], lambda o: solr.at[l, o, part_h], sem_x.at[0, l, h], sem_x.at[1, l, h]
            )

    def finish_wait(l):
        for h in range(2):
            for k in (1, 0):
                wait_bytes(solr.at[l, pl.ds(0, NR - 1), pl.ds(2 * h, 2)], sem_x.at[k, l, h])

    def emit(l):
        sol_out[l] = solr[l].reshape(SUP, 8, 128)

    def finish_all(l):
        for c in range(OWN):
            finish(l, c)

    def send_down(l):
        bwd_pack_send(l, 0, lambda k: solr[l + 1, k // OWN, pl.ds(k % OWN, 1)])

    def beside(l, t):
        if l == 0:
            if t < 2:
                convert(1, 16 * t, 16 * t + 16)
            else:
                partial_sums(3, 16 * t - 32, 16 * t - 16)
        elif l == 1:
            if t < 2:
                convert(2, 16 * t, 16 * t + 16)
            elif t == 2:
                ring_step(3, 2)
                fwd_collect(0, 1)
            else:
                fwd_collect(0, 2)

                @pl.loop(0, SUP)
                def _(g):
                    car_at(2, g, 7, 8)[...] = jnp.zeros((1, 8, 128), F32)
        else:
            if t < 2:
                partial_sums(2, 16 * t, 16 * t + 16)
            elif t == 2:
                fwd_collect(1, 1)
            else:
                fwd_collect(1, 2)

    def relay(l, g):
        a, b = BWD_GROUPS[l][g]
        bwd_pack_send(l, g, lambda k: anct[l + 1, k, pl.ds(a - 1, b - a)])

    pack_rhs(0)
    rsend[0] = rhs[0].reshape(NR, OWN, 8, 128)
    r_send(0)
    dinv_send(0)
    cum[SLOTS] = jnp.zeros(cum.shape[1:], F32)
    ids_send()
    for r in range(9, 16):
        arrv[r : r + 1, :] = jnp.zeros((1, 128), jnp.int32)

    @pl.loop(0, SUP)
    def _(g):
        car[g, 7] = jnp.zeros((8, 128), F32)
        for l in range(3):
            anct[l, g, 0] = jnp.zeros((8, 128), F32)
    for b in range(SUP // 8):
        pack_anc(b)
    ids_wait()
    bwd_pack_send(2, 1, lambda k: anc[k, pl.ds(0, 7)])
    convert(0)
    convert(3)
    for l in range(1, LEVELS):
        pack_rhs(l)
    dinv_wait(0)
    for l in range(LEVELS - 1):
        solve(l)
        spread_solved(l, functools.partial(beside, l))
        fwd_pack_send(l, 0)
        dinv_send(l + 1)
        ring_step(3, (1, 3, 4)[l])
        fwd_pack_send(l, 1)
        fwd_collect(l, 0)
        r_send(l + 1)
        p0_send(l)
        if l == 0:
            fwd_pack_send(0, 2)
            fwd_pack_send(0, 3)
            bwd_gather(2, 1)
            relay(1, 2)
            fwd_pack_send(0, 4)
        if l == 1:
            fwd_collect(0, 3)
            fwd_pack_send(1, 2)
            fwd_collect(0, 4)
            fwd_pack_send(1, 3)
            relay(1, 3)
            relay(1, 4)
        if l == 2:
            bwd_gather(1, 2)
            relay(0, 3)
        dinv_wait(l + 1)

    ring_step(2, 1)
    ring_end(3)
    solve(3)
    finish_all(3)
    bwd_gather(1, 3)
    relay(0, 4)
    ring_step(2, 2)
    p0_wait(2)
    finish_wait(3)
    send_down(2)
    fwd_pack_send(0, 5)
    ring_step(2, 3)
    spread_step(3, 0)
    p0_wait(1)
    emit(3)
    spread_step(3, 1)

    a_send(2)
    bwd_pack_send(1, 1, lambda k: asend[2, k // OWN, pl.ds(k % OWN, 1)])
    bwd_gather(1, 4)
    relay(0, 5)
    ring_step(2, 4)
    spread_step(3, 2)
    ring_end(2)
    a_wait(2)
    finish_all(2)
    p0_wait(0)
    fwd_collect(0, 5)
    fwd_pack_send(1, 4)
    bwd_gather(1, 1)
    partial_sums(1, 0, SUP)
    ring_step(1, 1)
    finish_wait(2)
    send_down(1)
    fwd_pack_send(1, 5)
    ring_step(1, 2)
    emit(2)
    ring_step(1, 3)

    a_send(1)
    bwd_pack_send(0, 1, lambda k: asend[1, k // OWN, pl.ds(k % OWN, 1)])
    relay(0, 2)
    fwd_collect(1, 3)
    fwd_pack_send(2, 2)
    ring_step(1, 4)
    bwd_gather(0, 3)
    bwd_gather(0, 4)
    ring_end(1)
    a_wait(1)
    finish_all(1)
    bwd_gather(0, 5)
    bwd_gather(0, 1)
    bwd_gather(0, 2)
    partial_sums(0, 0, SUP)
    ring_step(0, 1)
    finish_wait(1)
    send_down(0)
    fwd_collect(1, 4)
    fwd_pack_send(2, 3)
    ring_step(0, 2)
    fwd_collect(1, 5)
    fwd_pack_send(2, 4)
    fwd_pack_send(2, 5)
    emit(1)
    ring_step(0, 3)

    a_send(0)
    ring_step(0, 4)
    spread_step(3, 3)
    ring_end(0)
    a_wait(0)
    finish_all(0)
    spread_step(3, 4)
    for g in range(1, 6):
        fwd_collect(2, g)

    @pl.loop(0, SUP)
    def _(g):
        bu_out[g, pl.ds(0, 7)] = out_at(3, g, 0, 7)[...] + car_at(3, g, 0, 7)[...]
        bu_out[g, pl.ds(7, 1)] = out_at(3, g, 7, 8)[...]
    finish_wait(0)
    emit(0)


def tables(parent_owner, parent_local, ncol):
    cap = SLOTS // ncol
    owner = parent_owner[:, :, 0]
    here = jnp.arange(SUP, dtype=jnp.int32)
    same = (owner[:, :, None] == owner[:, None, :]) & (here[None, :, None] < here[None, None, :])
    pos = owner * cap + jnp.sum(same.astype(jnp.int32), axis=1)
    slots = jnp.arange(SLOTS, dtype=jnp.int32)
    hit = pos[:, None, :] == slots[None, :, None]
    fsrc = jnp.sum(jnp.where(hit, here[None, None, :], 0), axis=2)
    ids = jnp.sum(jnp.where(hit, parent_local[:, None, :] + 1, 0), axis=2)
    ids = ids.reshape(3, ncol, cap).transpose(1, 0, 2).reshape(ncol, 3 * cap)
    ids = jnp.pad(ids, ((0, 0), (0, 8 - 3 * cap)))
    ids = jnp.broadcast_to(ids[:, :, None], (ncol, 8, 128))
    wide = lambda x: jnp.pad(x, ((0, 0), (0, SLOTS - x.shape[1])))
    return jnp.stack([fsrc, wide(pos)], axis=1), ids


def per_device(ncol, rhs, dinv, panels, pattern, parent_owner, parent_local, ancestor_solution):
    tab, ids = tables(parent_owner, parent_local, ncol)
    vmem = pl.BlockSpec(memory_space=pltpu.VMEM)
    smem = pl.BlockSpec(memory_space=pltpu.SMEM)
    anywhere = pl.BlockSpec(memory_space=pl.ANY)
    sems = pltpu.SemaphoreType.DMA
    tile = (8, 128)
    fsend = tuple(pltpu.VMEM((SLOTS, b - a) + tile, F32) for a, b in FWD_GROUPS)
    frecv = tuple(pltpu.VMEM((2, SLOTS, b - a) + tile, F32) for a, b in FWD_GROUPS)
    bbuf = tuple(tuple(pltpu.VMEM((SLOTS, b - a) + tile, F32) for a, b in groups) for groups in BWD_GROUPS)
    sol, bu = pl.pallas_call(
        functools.partial(kernel, ncol),
        out_shape=(
            jax.ShapeDtypeStruct((LEVELS, SUP) + tile, F32),
            jax.ShapeDtypeStruct((SUP, ANC) + tile, F32),
        ),
        in_specs=[smem, smem, vmem, anywhere, anywhere, anywhere, anywhere],
        out_specs=(vmem, vmem),
        scratch_shapes=[
            pltpu.VMEM((LEVELS, SUP) + tile, F32),
            pltpu.VMEM((SUP, ANC) + tile, F32),
            pltpu.VMEM((2, 16, SUP, 64), F32),
            pltpu.VMEM((2, 16, 8, ANC, 64), F32),
            sems((2, 2)),
            pltpu.VMEM((32,) + tile, jnp.int32),
            pltpu.VMEM((16, 128), jnp.int32),
            pltpu.SMEM((16, 128), jnp.int32),
            pltpu.VMEM((2, ANC, SUP, 16, 128), F32),
            pltpu.VMEM((LEVELS, SUP, 128, 256), BF16),
            pltpu.VMEM((LEVELS, SUP, 128, 256), BF16),
            pltpu.VMEM((LEVELS, NR, OWN, 16, 128), F32),
            pltpu.VMEM((LEVELS, OWN, 128, 256), BF16),
            pltpu.VMEM((LEVELS, OWN, 128, 256), BF16),
            pltpu.VMEM((3, NR, OWN, 16, 128), F32),
            pltpu.VMEM((3, OWN, 128, 256), BF16),
            pltpu.VMEM((LEVELS, NR, OWN) + tile, F32),
            pltpu.VMEM((LEVELS, NR, OWN) + tile, F32),
            pltpu.VMEM((3, NR, OWN) + tile, F32),
            pltpu.VMEM((3, NR, OWN) + tile, F32),
            pltpu.VMEM((LEVELS, OWN, 64, 128), F32),
            pltpu.VMEM((2, NR, OWN, 64, 128), F32),
            pltpu.VMEM((2, SUP, ANC) + tile, F32),
            pltpu.VMEM((SUP, ANC) + tile, F32),
            pltpu.VMEM((SLOTS + 1, 2) + tile, F32),
            fsend, frecv, pltpu.VMEM((3, 3, SLOTS, 1) + tile, F32), pltpu.VMEM((SLOTS, 7) + tile, F32), bbuf,
            pltpu.VMEM((3, SUP, ANC) + tile, F32),
            pltpu.VMEM((2, NR, OWN, 64, 128), F32),
            pltpu.VMEM((2, 2, 4, OWN, 64, 128), F32),
            pltpu.VMEM((OWN, 64, 128), F32),
            pltpu.VMEM((LEVELS, NR, OWN) + tile, F32),
            pltpu.VMEM((LEVELS, NR, OWN) + tile, F32),
            sems((3,)), sems((2,)), sems((3, LEVELS)), sems((3, 3)), sems((2, 3)), sems((2, LEVELS, 2)),
            sems((LEVELS, OWN, 4, 2)), sems((LEVELS, OWN, 4, 2)),
            sems((3, 6)), sems((3, 6)), sems((3, 6)), sems((3, 6)),
            sems((LEVELS, OWN, 4, 2)), sems((LEVELS, OWN, 4, 2)), sems((2, LEVELS, 2)),
        ],
        compiler_params=pltpu.CompilerParams(
            collective_id=0, has_side_effects=True, vmem_limit_bytes=62 * 1024 * 1024
        ),
        cost_estimate=pl.CostEstimate(flops=4 * 10**9, bytes_accessed=12 * 10**6, transcendentals=0),
    )(tab, pattern, ids, rhs, ancestor_solution, dinv, panels)
    solution = sol.reshape(LEVELS, SUP, 8, 2, 64).transpose(0, 3, 2, 1, 4).reshape(LEVELS, 16, SUP, 64)
    boundary = bu.reshape(SUP, ANC, 8, 2, 64).transpose(3, 2, 0, 1, 4).reshape(16, SUP, ANC, 64)
    return solution, boundary


def solution(mesh):
    placed = (
        P(None, "row", "col", None),
        P(None, "col", "row", None),
        P(None, None, "col", "row", None),
        P(None, None, "col"),
        P(None, "col", None),
        P(None, "col"),
        P("row", "col", None, None),
    )
    return jax.shard_map(
        functools.partial(per_device, mesh.shape["col"]),
        mesh=mesh,
        in_specs=placed,
        out_specs=(P(None, "row", "col", None), P("row", "col", None, None)),
        check_vma=False,
    )
```
